512 devices in a mesh: inst: 32 (over z, core), tp: 16 (over x, y).
Axes of the slice: x: 4, y: 4, z: 16, core: 2. Of those that a mesh axis runs over, the one named last changes fastest.
Arguments:
- queries: bfloat16 [512, 8192], P('inst', 'tp'), may hold values from -5 to 5, as said below
- home_keys: bfloat16 [8192, 16, 1024], P(('inst', 'tp')), may hold values from -5 to 5
- home_values: bfloat16 [8192, 16, 1024], P(('inst', 'tp')), may hold values from -12 to 12
- home_table: int32 [512, 16, 1], P('inst', 'tp'), may hold values from 0 to 15
- home_len: int32 [512, 16], P('inst', 'tp'), may hold values from 2 to 16
- lent_keys: bfloat16 [16384, 16, 1024], P(('inst', 'tp')), may hold values from -5 to 5
- lent_values: bfloat16 [16384, 16, 1024], P(('inst', 'tp')), may hold values from -12 to 12
- lend_row: int32 [32, 32, 16, 2], P('inst', None, 'tp'), may hold values from 0 to 15
- lend_table: int32 [32, 32, 16, 2, 2], P('inst', None, 'tp'), may hold values from 0 to 31
- lend_len: int32 [32, 32, 16, 2], P('inst', None, 'tp'), may hold values from 0 to 32, as said below
Outputs:
- attended: bfloat16 [512, 8192], P('inst', 'tp')
The draws below stay inside these ranges and needn't reach their ends.
Inputs may be any that keep to these rules, and one draw needn't show every extreme that they name: `queries`: hidden draws take other laws within the same range. `lend_len`: live slots hold 2 or more tokens; every creditor has a slot of exactly 32 tokens; creditors' loads differ.
All inputs are finite; a program needn't handle non-finite values.
Results may differ from the reference program's by a relative error of at most 0.004.
Values may be sent and summed in bfloat16 or wider, within the bound.
No kernel may reach another device: no remote copies, remote signals or barrier semaphores. Data moves between devices by JAX's collectives and lax.ppermute only.
A program may use at most 64 MiB of HBM per device.

```python
import jax
import jax.numpy as jnp
from jax import lax

QH = 64
KVH = 8
HD = 128
BS = 16
ROWS = 16
HB = 1
LB = 2
CAP = 2
LPOOL = 32
HPOOL = 16
ROWS_ALL = 512
SLOTS_HOME = 8192
SLOTS_LENT = 16384
N_INST = 32
N_TP = 16


def pool_keys(key, slots, salt):
    key = jax.random.fold_in(key, salt)
    base = jnp.clip(jax.random.normal(key, (slots, BS, KVH, HD), jnp.float32), -5.0, 5.0)
    return base.reshape(slots, BS, KVH * HD).astype(jnp.bfloat16)


def draw_home_keys(key, part):
    return pool_keys(key, SLOTS_HOME, 11)


def draw_lent_keys(key, part):
    return pool_keys(key, SLOTS_LENT, 13)


def draw_queries(key, part):
    key = jax.random.fold_in(key, 17)
    first = jax.random.fold_in(key, 0)
    base = jnp.clip(jax.random.normal(first, (ROWS_ALL, QH * HD), jnp.float32), -5.0, 5.0)
    return base.astype(jnp.bfloat16)


def draw_lend_len(key, part):
    key = jax.random.fold_in(key, 7)
    first, second, third, fourth = jax.random.split(key, 4)
    shape = (N_INST, N_INST, N_TP, CAP)
    level = jax.random.randint(first, (N_INST, 1, 1, 1), 0, 4)
    live = jax.random.randint(second, shape, 0, 16) < (level + 1) * (level + 1)
    length = jax.random.randint(third, shape, 2, LB * BS + 1)
    pick = jax.random.randint(fourth, (N_INST,), 0, N_INST)
    owner = jnp.arange(N_INST)[None, :, None, None] == pick[:, None, None, None]
    corner = (jnp.arange(N_TP)[None, None, :, None] == 0) & (jnp.arange(CAP)[None, None, None, :] == 0)
    force = owner & corner
    length = jnp.where(force, LB * BS, length)
    live = live | force
    return jnp.where(live, length, 0).astype(jnp.int32)


def place_ends(entries, own_key, least, high):
    place = [jax.random.randint(jax.random.fold_in(own_key, axis), (), 0, length) for axis, length in enumerate(entries.shape)]
    longest = entries.shape.index(max(entries.shape))
    neighbour = place[:longest] + [(place[longest] + 1) % entries.shape[longest]] + place[longest + 1:]
    return entries.at[tuple(place)].set(least).at[tuple(neighbour)].set(high)


def levels(key, extent, cuts, low, high):
    loudness = 1.0
    for dim, blocks in cuts:
        steps = jax.random.uniform(jax.random.fold_in(jax.random.fold_in(key, 6), dim), (blocks,), jnp.float32, low / len(cuts), high / len(cuts))
        loudness = loudness * jnp.repeat(jnp.exp(steps), extent[dim] // blocks).reshape((-1,) + (1,) * (len(extent) - 1 - dim))
    return loudness


def scatter_about(key, shape, width, most, cuts=(), kind=jnp.bfloat16):
    gain = levels(key, shape, cuts, -0.22, 0.18) if cuts else 1.0
    result = jax.random.normal(key, shape, jnp.float32) * width * gain
    return jnp.minimum(jnp.maximum(result, -most), most).astype(kind)


def setup_inputs(seed: int = 0) -> dict:
    key_list = jax.random.split(jax.random.key(seed), 11)
    queries = draw_queries(jax.random.fold_in(key_list[10], 71), 0)
    home_keys = draw_home_keys(jax.random.fold_in(key_list[10], 71), 0)
    home_values = scatter_about(key_list[2], (SLOTS_HOME, BS, KVH * HD), 2.0, 12.0, ((0, 512),))
    home_table = place_ends(jax.random.randint(key_list[3], (ROWS_ALL, N_TP, HB), 0, HPOOL), jax.random.fold_in(key_list[3], 1), 0, HPOOL - 1).astype(jnp.int32)
    home_len = place_ends(jax.random.randint(key_list[4], (ROWS_ALL, N_TP), 2, HB * BS + 1), jax.random.fold_in(key_list[4], 1), 2, HB * BS).astype(jnp.int32)
    lent_keys = draw_lent_keys(jax.random.fold_in(key_list[10], 71), 0)
    lent_values = scatter_about(key_list[6], (SLOTS_LENT, BS, KVH * HD), 2.0, 12.0, ((0, 512),))
    lend_row = place_ends(jax.random.randint(key_list[7], (N_INST, N_INST, N_TP, CAP), 0, ROWS), jax.random.fold_in(key_list[7], 1), 0, ROWS - 1).astype(jnp.int32)
    lend_table = place_ends(jax.random.randint(key_list[8], (N_INST, N_INST, N_TP, CAP, LB), 0, LPOOL), jax.random.fold_in(key_list[8], 1), 0, LPOOL - 1).astype(jnp.int32)
    lend_len = draw_lend_len(jax.random.fold_in(key_list[10], 71), 0)
    return {"queries": queries, "home_keys": home_keys, "home_values": home_values, "home_table": home_table, "home_len": home_len, "lent_keys": lent_keys, "lent_values": lent_values, "lend_row": lend_row, "lend_table": lend_table, "lend_len": lend_len}


def attend(query, keys, values, length):
    scores = jnp.einsum("rkgd,rskd->rkgs", query.astype(jnp.float32), keys.astype(jnp.float32)) * (HD ** -0.5)
    live = jnp.arange(keys.shape[1], dtype=jnp.int32)[None, None, None, :] < length[:, None, None, None]
    peak = jnp.max(jnp.where(live, scores, -jnp.inf), axis=3)
    weights = jnp.where(live, jnp.exp(scores - peak[..., None]), 0.0).astype(jnp.bfloat16)
    total = jnp.sum(weights.astype(jnp.float32), axis=3)
    mixed = jnp.einsum("rkgs,rskd->rkgd", weights.astype(jnp.float32), values.astype(jnp.float32)) / total[..., None]
    return mixed, peak + jnp.log(total)


def reference(queries, home_keys, home_values, home_table, home_len, lent_keys, lent_values, lend_row, lend_table, lend_len):
    group = QH // KVH
    query_flat = queries.reshape(ROWS_ALL, KVH, group, HD)
    tp_index = jnp.arange(N_TP, dtype=jnp.int32)

    def home_one(xs):
        query, table, length, inst = xs
        slots = ((inst * N_TP + tp_index[None, :, None]) * HPOOL + table).astype(jnp.int32)
        keys = home_keys[slots].reshape(ROWS * N_TP, HB * BS, KVH, HD)
        values = home_values[slots].reshape(ROWS * N_TP, HB * BS, KVH, HD)
        spread = jnp.broadcast_to(query[:, None], (ROWS, N_TP, KVH, group, HD)).reshape(ROWS * N_TP, KVH, group, HD)
        mixed, lse = attend(spread, keys, values, length.reshape(-1))
        mixed = mixed.reshape(ROWS, N_TP, KVH, group, HD)
        lse = lse.reshape(ROWS, N_TP, KVH, group)
        peak = jnp.max(lse, axis=1)
        weight = jnp.exp(lse - peak[:, None])
        return peak, jnp.sum(weight, axis=1), jnp.sum(weight[..., None] * mixed, axis=1)

    peak, total, summed = lax.map(home_one, (query_flat.reshape(N_INST, ROWS, KVH, group, HD), home_table.reshape(N_INST, ROWS, N_TP, HB), home_len.reshape(N_INST, ROWS, N_TP), jnp.arange(N_INST, dtype=jnp.int32)))
    peak = peak.reshape(ROWS_ALL, KVH, group)
    total = total.reshape(ROWS_ALL, KVH, group)
    summed = summed.reshape(ROWS_ALL, KVH, group, HD)

    def lend_step(carry, xs):
        peak, total, summed = carry
        table, length, rows_local, creditor = xs
        slots = ((creditor * N_TP + tp_index[None, :, None, None]) * LPOOL + table).astype(jnp.int32)
        count = N_INST * N_TP * CAP
        keys = lent_keys[slots].reshape(count, LB * BS, KVH, HD)
        values = lent_values[slots].reshape(count, LB * BS, KVH, HD)
        row_ids = (jnp.arange(N_INST, dtype=jnp.int32)[:, None, None] * ROWS + rows_local).reshape(-1).astype(jnp.int32)
        flat_len = length.reshape(-1)
        mixed, lse = attend(query_flat[row_ids], keys, values, jnp.maximum(flat_len, 1))
        live = (flat_len > 0)[:, None, None]
        new_peak = peak.at[row_ids].max(jnp.where(live, lse, -jnp.inf))
        weight = jnp.where(live, jnp.exp(lse - new_peak[row_ids]), 0.0)
        rescale = jnp.exp(peak - new_peak)
        total = (total * rescale).at[row_ids].add(weight)
        summed = (summed * rescale[..., None]).at[row_ids].add(weight[..., None] * mixed)
        return (new_peak, total, summed), None

    (peak, total, summed), unused = lax.scan(lend_step, (peak, total, summed), (lend_table, lend_len, jnp.transpose(lend_row, (1, 0, 2, 3)), jnp.arange(N_INST, dtype=jnp.int32)))
    return (summed / total[..., None]).reshape(ROWS_ALL, QH * HD).astype(jnp.bfloat16)
```

```python
import functools
import math

import jax
import jax.numpy as jnp
from jax import lax
from jax.experimental import pallas as pl
from jax.experimental.pallas import tpu as pltpu
from jax.sharding import PartitionSpec as P

QH = 64
KVH = 8
HD = 128
N_INST = 32
N_TP = 16
ROWS = 16
SLOTS = 64
WIDTH = 512
GROUPS = 4
SEGS = SLOTS + ROWS
DEAD = -1e30
SCALE = HD ** (-0.5)
F32 = jnp.float32
BF16 = jnp.bfloat16


def iota(shape, axis):
    return lax.broadcasted_iota(jnp.int32, shape, axis)


def dot(a, b):
    return jnp.dot(a, b, preferred_element_type=F32)


def dot_nt(a, b):
    return lax.dot_general(a, b, (((1,), (1,)), ((), ())), preferred_element_type=F32)


def split3(x):
    hi = x.astype(BF16).astype(F32)
    rest = x - hi
    mid = rest.astype(BF16).astype(F32)
    return hi, mid, rest - mid


def spread3(x):
    hi, mid, low = split3(x)
    return hi + pltpu.roll(mid, 4, 1) + pltpu.roll(low, 8, 1)


def pick_kernel(me_ref, all_ref, out_ref, target_ref):
    me = me_ref[0]
    k = iota((256, 128), 0)
    n = iota((256, 128), 1)
    local = jnp.bitwise_and(jnp.right_shift(k, 1), 7)
    order = jnp.where(n == local * 16 + jnp.right_shift(k, 4), 1.0, 0.0).astype(BF16)
    second = jnp.bitwise_and(k, 1) == 1
    base = local.astype(F32) * 16.0
    lane = n.astype(F32)
    row = iota((128, 128), 0)
    for g in range(GROUPS):
        rows = pl.ds(g * 128, 128)
        asked = all_ref[rows, WIDTH:]
        found = []
        for s in range(2):
            column = jnp.where(row == 2 * me + s, 1.0, 0.0).astype(BF16)
            found.append(dot(order, dot(asked, column).astype(BF16)))
        target = jnp.where(second, found[1], found[0]) + base
        onehot = jnp.where(lane == target, 1.0, 0.0).astype(BF16)
        picked = dot(onehot, all_ref[rows, :WIDTH]).astype(BF16)
        out_ref[:, g * 16 : (g + 1) * 16, :] = picked.reshape(N_TP, 16, WIDTH)
        target_ref[g] = target.T[:8]
    own = all_ref[pl.ds(pl.multiple_of(me * ROWS, ROWS), ROWS), :WIDTH]
    for t in range(N_TP):
        out_ref[t, SLOTS:, :] = own


def attend_kernel(
    lent_ref, home_ref, x_ref, lk_ref, lv_ref, hk_ref, hv_ref, out_ref, count_s, bias_s, hbias_s
):
    @pl.when(pl.program_id(0) == 0)
    def _():
        token = iota((SLOTS, 512), 1)
        block = jnp.right_shift(token, 4)
        place = jnp.bitwise_and(token, 15)
        length = lent_ref[:, 2:3]
        first = (block == lent_ref[:, 0:1]) & (place < length)
        other = (block == lent_ref[:, 1:2]) & (place + 16 < length)
        count = jnp.where(first, 1.0, 0.0) + jnp.where(other, 1.0, 0.0)
        count_s[...] = count
        bias_s[...] = jnp.where(count > 0, 0.0, DEAD)
        token = iota((ROWS, 256), 1)
        live = (jnp.right_shift(token, 4) == home_ref[:, 0:1]) & (
            jnp.bitwise_and(token, 15) < home_ref[:, 1:2]
        )
        hbias_s[...] = jnp.where(live, 0.0, DEAD)

    factor = SCALE * math.log2(math.e)
    lent_k = lk_ref[...].reshape(512, HD)
    lent_v = lv_ref[...].reshape(512, HD)
    home_k = hk_ref[...].reshape(256, HD)
    home_v = hv_ref[...].reshape(256, HD)
    lane = iota((SLOTS, 128), 1)
    hlane = iota((ROWS, 128), 1)
    for tt in range(2):
        query = jnp.concatenate(
            [x_ref[tt, :SLOTS, h * HD : (h + 1) * HD] for h in range(4)], axis=0
        )
        scores = dot_nt(query, lent_k)
        lse = jnp.zeros((SLOTS, 128), F32)
        weights = []
        totals = []
        for h in range(4):
            part = scores[h * SLOTS : (h + 1) * SLOTS] + bias_s[...]
            peak = jnp.max(part, axis=1, keepdims=True)
            weight = (jnp.exp2((part - peak) * factor) * count_s[...]).astype(BF16)
            total = jnp.sum(weight.astype(F32), axis=1, keepdims=True)
            live = total > 0
            total = jnp.where(live, total, 1.0)
            lse = jnp.where(
                lane == h, jnp.where(live, peak * SCALE + jnp.log(total), DEAD), lse
            )
            weights.append(weight)
            totals.append(total)
        mixed = dot(jnp.concatenate(weights, axis=0), lent_v)
        for h in range(4):
            out_ref[tt, :SLOTS, h * HD : (h + 1) * HD] = (
                mixed[h * SLOTS : (h + 1) * SLOTS] / totals[h]
            ).astype(BF16)
        query = jnp.concatenate(
            [x_ref[tt, SLOTS:, h * HD : (h + 1) * HD] for h in range(4)], axis=0
        )
        scores = dot_nt(query, home_k)
        hlse = jnp.zeros((ROWS, 128), F32)
        weights = []
        totals = []
        for h in range(4):
            part = scores[h * ROWS : (h + 1) * ROWS] + hbias_s[...]
            peak = jnp.max(part, axis=1, keepdims=True)
            weight = jnp.exp2((part - peak) * factor).astype(BF16)
            total = jnp.sum(weight.astype(F32), axis=1, keepdims=True)
            hlse = jnp.where(hlane == h, peak * SCALE + jnp.log(total), hlse)
            weights.append(weight)
            totals.append(total)
        mixed = dot(jnp.concatenate(weights, axis=0), home_v)
        for h in range(4):
            out_ref[tt, SLOTS:SEGS, h * HD : (h + 1) * HD] = (
                mixed[h * ROWS : (h + 1) * ROWS] / totals[h]
            ).astype(BF16)
        column = jnp.concatenate([lse, hlse, jnp.zeros((128 - SEGS, 128), F32)], axis=0)
        out_ref[tt, SEGS:, :128] = spread3(column).T[:16].astype(BF16)
        out_ref[tt, SEGS:, 128:] = jnp.zeros((16, WIDTH - 128), BF16)


def merge_kernel(target_ref, x_ref, lent_ref, home_ref):
    lane = iota((8, 128), 1)
    lses = []
    for t in range(N_TP):
        parts = x_ref[t, SEGS:, :128].astype(F32)
        lses.append(parts[0:4] + parts[4:8] + parts[8:12])
    lses = [jnp.concatenate([x, x], axis=0) for x in lses]
    for g in range(GROUPS + 1):
        halves = []
        for half in range(2):
            row = jnp.zeros((8, 128), F32)
            for j in range(8):
                shift = (16 * j - 16 * g) % 128
                moved = lses[half * 8 + j]
                moved = pltpu.roll(moved, shift, 1) if shift else moved
                row = jnp.where(jnp.right_shift(lane, 4) == j, moved, row)
            halves.append(row)
        lse = jnp.concatenate(halves, axis=1)
        high = 128 if g < GROUPS else ROWS
        rows = iota((high, 256), 0)
        if g < GROUPS:
            mask = rows.astype(F32) == target_ref[g, 0:1, :]
        else:
            mask = rows == jnp.bitwise_and(iota((high, 256), 1), 15)
        values = x_ref[:, g * 16 : (g + 1) * 16, :].reshape(256, WIDTH)
        out_lse = jnp.zeros((high, 128), F32)
        out_lane = iota((high, 128), 1)
        mixed = []
        for h in range(4):
            score = jnp.where(mask, lse[h : h + 1, :], DEAD)
            peak = jnp.max(score, axis=1, keepdims=True)
            weight = jnp.exp(score - peak)
            total = jnp.sum(weight, axis=1, keepdims=True)
            upper = weight.astype(BF16)
            lower = (weight - upper.astype(F32)).astype(BF16)
            both = dot(
                jnp.concatenate([upper, lower], axis=0), values[:, h * HD : (h + 1) * HD]
            )
            mixed.append((both[:high] + both[high:]) / total)
            out_lse = jnp.where(out_lane == h, peak + jnp.log(total), out_lse)
        if g < GROUPS:
            block = slice(g * 8, (g + 1) * 8)
            for h in range(4):
                lent_ref[block, :, h * HD : (h + 1) * HD] = (
                    mixed[h].astype(BF16).reshape(8, ROWS, HD)
                )
            lent_ref[block, :, WIDTH:] = (
                spread3(out_lse).astype(BF16).reshape(8, ROWS, 128)
            )
        else:
            for h in range(4):
                home_ref[:, h * HD : (h + 1) * HD] = mixed[h]
            home_ref[:, WIDTH:] = out_lse


def final_kernel(home_ref, x_ref, out_ref):
    pieces = x_ref.shape[0]
    lses = [home_ref[:, WIDTH:]]
    for c in range(pieces):
        parts = x_ref[c, :, WIDTH:].astype(F32)
        lses.append(parts + pltpu.roll(parts, 124, 1) + pltpu.roll(parts, 120, 1))
    peak = functools.reduce(jnp.maximum, lses)
    weights = [jnp.exp(lse - peak) for lse in lses]
    total = sum(weights)
    for h in range(4):
        cut = slice(h * HD, (h + 1) * HD)
        mixed = weights[0][:, h : h + 1] * home_ref[:, cut]
        for c in range(pieces):
            mixed = mixed + weights[c + 1][:, h : h + 1] * x_ref[c, :, cut].astype(F32)
        out_ref[:, cut] = (mixed / total[:, h : h + 1]).astype(BF16)


VMEM = pl.BlockSpec(memory_space=pltpu.VMEM)
SMEM = pl.BlockSpec(memory_space=pltpu.SMEM)
PARAMS = pltpu.CompilerParams(vmem_limit_bytes=48 * 1024 * 1024)


def exchange(x, axis):
    return lax.all_to_all(x, axis, split_axis=0, concat_axis=0, tiled=True)


def per_device(
    queries,
    home_keys,
    home_values,
    home_table,
    home_len,
    lent_keys,
    lent_values,
    lend_row,
    lend_table,
    lend_len,
):
    me = lax.axis_index("inst").astype(jnp.int32).reshape(1)
    asked = exchange(jnp.broadcast_to(lend_row.reshape(1, SLOTS), (N_TP, SLOTS)), "tp")
    sent = jnp.concatenate(
        [queries, asked.astype(BF16), jnp.zeros((ROWS, 128 - SLOTS), BF16)], axis=1
    )
    gathered = lax.all_gather(sent, "inst", axis=0, tiled=True)
    picked, target = pl.pallas_call(
        pick_kernel,
        out_shape=(
            jax.ShapeDtypeStruct((N_TP, SEGS, WIDTH), BF16),
            jax.ShapeDtypeStruct((GROUPS, 8, 256), F32),
        ),
        in_specs=[SMEM, VMEM],
        out_specs=(VMEM, VMEM),
        compiler_params=PARAMS,
        name="pick",
    )(me, gathered)
    arrived = exchange(picked, "tp")
    lent_meta = jnp.concatenate(
        [lend_table.reshape(SLOTS, 2), lend_len.reshape(SLOTS, 1)], axis=1
    )
    home_meta = jnp.concatenate([home_table.reshape(ROWS, 1), home_len], axis=1)
    partial = pl.pallas_call(
        attend_kernel,
        grid=(KVH,),
        out_shape=jax.ShapeDtypeStruct((N_TP, SEGS + 16, WIDTH), BF16),
        in_specs=[
            pl.BlockSpec((SLOTS, 3), lambda k: (0, 0)),
            pl.BlockSpec((ROWS, 2), lambda k: (0, 0)),
            pl.BlockSpec((2, SEGS, WIDTH), lambda k: (k, 0, 0)),
            pl.BlockSpec((32, 16, HD), lambda k: (0, 0, k)),
            pl.BlockSpec((32, 16, HD), lambda k: (0, 0, k)),
            pl.BlockSpec((16, 16, HD), lambda k: (0, 0, k)),
            pl.BlockSpec((16, 16, HD), lambda k: (0, 0, k)),
        ],
        out_specs=pl.BlockSpec((2, SEGS + 16, WIDTH), lambda k: (k, 0, 0)),
        scratch_shapes=[
            pltpu.VMEM((SLOTS, 512), F32),
            pltpu.VMEM((SLOTS, 512), F32),
            pltpu.VMEM((ROWS, 256), F32),
        ],
        compiler_params=PARAMS,
        name="attend",
    )(lent_meta, home_meta, arrived, lent_keys, lent_values, home_keys, home_values)
    returned = exchange(partial, "tp")
    lent, home = pl.pallas_call(
        merge_kernel,
        out_shape=(
            jax.ShapeDtypeStruct((N_INST, ROWS, WIDTH + 128), BF16),
            jax.ShapeDtypeStruct((ROWS, WIDTH + 128), F32),
        ),
        in_specs=[VMEM, VMEM],
        out_specs=(VMEM, VMEM),
        compiler_params=PARAMS,
        name="merge",
    )(target, returned)
    back = exchange(lent, "inst")
    return pl.pallas_call(
        final_kernel,
        out_shape=jax.ShapeDtypeStruct((ROWS, WIDTH), BF16),
        in_specs=[VMEM, VMEM],
        out_specs=VMEM,
        compiler_params=PARAMS,
        name="final",
    )(home, back)


def solution(mesh):
    in_specs = (
        P("inst", "tp"),
        P(("inst", "tp"), None, None),
        P(("inst", "tp"), None, None),
        P("inst", "tp", None),
        P("inst", "tp"),
        P(("inst", "tp"), None, None),
        P(("inst", "tp"), None, None),
        P("inst", None, "tp", None),
        P("inst", None, "tp", None, None),
        P("inst", None, "tp", None),
    )
    out_specs = P("inst", "tp")
    return jax.shard_map(
        per_device, mesh=mesh, in_specs=in_specs, out_specs=out_specs, check_vma=False
    )
```

```python
import functools
import math

import jax
import jax.numpy as jnp
import ml_dtypes
import numpy as np
from jax import lax
from jax.experimental import pallas as pl
from jax.experimental.pallas import tpu as pltpu
from jax.sharding import PartitionSpec as P

QH = 64
KVH = 8
HD = 128
N_INST = 32
N_TP = 16
ROWS = 16
SLOTS = 64
WIDTH = 512
GROUPS = 4
SEGS = SLOTS + ROWS
DEAD = -1e30
SCALE = HD ** (-0.5)
F32 = jnp.float32
BF16 = jnp.bfloat16
FACTOR = SCALE * math.log2(math.e)
TWICE_HI = float(np.float32(1 / FACTOR).astype(ml_dtypes.bfloat16))
TWICE_LO = 1 / FACTOR - TWICE_HI
UNROLL = 2


def iota(shape, axis):
    return lax.broadcasted_iota(jnp.int32, shape, axis)


def dot(a, b):
    return jnp.dot(a, b, preferred_element_type=F32)


def dot_nt(a, b):
    return lax.dot_general(a, b, (((1,), (1,)), ((), ())), preferred_element_type=F32)


def split3(x):
    hi = x.astype(BF16).astype(F32)
    rest = x - hi
    mid = rest.astype(BF16).astype(F32)
    return hi, mid, rest - mid


def spread3(x):
    hi, mid, low = split3(x)
    return hi + pltpu.roll(mid, 4, 1) + pltpu.roll(low, 8, 1)


def pick_kernel(me_ref, mine_ref, other_ref, out_ref, target_ref):
    me = me_ref[0]
    k = iota((256, 128), 0)
    n = iota((256, 128), 1)
    local = jnp.bitwise_and(jnp.right_shift(k, 1), 7)
    order = jnp.where(n == local * 16 + jnp.right_shift(k, 4), 1.0, 0.0).astype(BF16)
    second = jnp.bitwise_and(k, 1) == 1
    base = local.astype(F32) * 16.0
    lane = n.astype(F32)
    row = iota((128, 128), 0)
    for g in range(GROUPS):
        source = mine_ref if g < 2 else other_ref
        block = source[(g % 2) * 8 : (g % 2 + 1) * 8].reshape(128, WIDTH + 128)
        asked = block[:, WIDTH:]
        found = []
        for s in range(2):
            column = jnp.where(row == 2 * me + s, 1.0, 0.0).astype(BF16)
            found.append(dot(order, dot(asked, column).astype(BF16)))
        target = jnp.where(second, found[1], found[0]) + base
        onehot = jnp.where(lane == target, 1.0, 0.0).astype(BF16)
        picked = dot(onehot, block[:, :WIDTH]).astype(BF16)
        out_ref[:, g * 16 : (g + 1) * 16, :] = picked.reshape(N_TP, 16, WIDTH)
        target_ref[g] = target.T[:8]
    own = mine_ref[jnp.right_shift(me, 1), :, :WIDTH]
    for t in range(N_TP):
        out_ref[t, SLOTS:, :] = own


def prepare_kernel(
    lent_ref, home_ref, lk_ref, lv_ref, hk_ref, hv_ref, klent_ref, vlent_ref, khome_ref, vhome_ref
):
    token = iota((512, 128), 0)
    block = jnp.right_shift(token, 4)
    place = jnp.bitwise_and(token, 15)
    length = lent_ref[2:3, :]
    first = (block == lent_ref[0:1, :]) & (place < length)
    other = (block == lent_ref[1:2, :]) & (place + 16 < length)
    twice = first & other
    upper = jnp.where(first | other, jnp.where(twice, TWICE_HI, 0.0), DEAD)
    lower = jnp.where(twice, TWICE_LO, 0.0)
    lent_mask = jnp.where(iota((512, 128), 1) < SLOTS, upper, lower).astype(BF16)
    token = iota((256, 128), 0)
    live = (jnp.right_shift(token, 4) == home_ref[0:1, :]) & (
        jnp.bitwise_and(token, 15) < home_ref[1:2, :]
    )
    home_mask = jnp.where(live, 0.0, DEAD).astype(BF16)
    ones = jnp.ones((512, 128), BF16)
    for k in range(KVH):
        cut = slice(k * HD, (k + 1) * HD)
        klent_ref[k, :, :HD] = lk_ref[:, :, cut].reshape(512, HD)
        klent_ref[k, :, HD:] = lent_mask
        vlent_ref[k, :, :HD] = lv_ref[:, :, cut].reshape(512, HD)
        vlent_ref[k, :, HD:] = ones
        khome_ref[k, :, :HD] = hk_ref[:, :, cut].reshape(256, HD)
        khome_ref[k, :, HD:] = home_mask
        vhome_ref[k, :, :HD] = hv_ref[:, :, cut].reshape(256, HD)
        vhome_ref[k, :, HD:] = ones[:256]


def attend_kernel(x_ref, klent_ref, vlent_ref, khome_ref, vhome_ref, out_ref):
    def pool(query, pick, keys, values, count):
        query = jnp.concatenate([query, jnp.concatenate([pick] * 8, axis=0)], axis=1)
        scores = dot_nt(query, keys)
        weights = []
        peaks = []
        for j in range(8):
            part = scores[j * count : (j + 1) * count]
            peak = jnp.max(part, axis=1, keepdims=True)
            weights.append(jnp.exp2((part - peak) * FACTOR).astype(BF16))
            peaks.append(peak)
        mixed = dot(jnp.concatenate(weights, axis=0), values)
        total = mixed[:, HD:]
        return (mixed[:, :HD] / total).astype(BF16), peaks, total

    def stack(k, rows):
        return jnp.concatenate(
            [
                x_ref[2 * k + tt, rows, h * HD : (h + 1) * HD]
                for tt in range(2)
                for h in range(4)
            ],
            axis=0,
        )

    def columns(tt, peaks, total, count):
        lane = iota((count, 128), 1)
        top = jnp.zeros((count, 128), F32)
        amount = jnp.ones((count, 128), F32)
        for h in range(4):
            j = tt * 4 + h
            top = jnp.where(lane == h, peaks[j], top)
            amount = jnp.where(lane == h, total[j * count : (j + 1) * count], amount)
        return jnp.where(top > DEAD / 2, top * SCALE + jnp.log(amount), DEAD)

    lane = iota((SLOTS, 128), 1)
    lent_pick = jnp.where(
        jnp.bitwise_and(lane, SLOTS - 1) == iota((SLOTS, 128), 0), 1.0, 0.0
    ).astype(BF16)
    home_pick = jnp.where(iota((ROWS, 128), 1) == iota((ROWS, 128), 0), 1.0, 0.0).astype(BF16)

    def step(k, carry):
        lent, lent_peaks, lent_total = pool(
            stack(k, slice(0, SLOTS)), lent_pick, klent_ref[k], vlent_ref[k], SLOTS
        )
        home, home_peaks, home_total = pool(
            stack(k, slice(SLOTS, SEGS)), home_pick, khome_ref[k], vhome_ref[k], ROWS
        )
        for tt in range(2):
            for h in range(4):
                j = tt * 4 + h
                at = h * SEGS
                out_ref[2 * k + tt, at : at + SLOTS, :] = lent[j * SLOTS : (j + 1) * SLOTS]
                out_ref[2 * k + tt, at + SLOTS : at + SEGS, :] = home[j * ROWS : (j + 1) * ROWS]
            column = jnp.concatenate(
                [
                    columns(tt, lent_peaks, lent_total, SLOTS),
                    columns(tt, home_peaks, home_total, ROWS),
                    jnp.zeros((128 - SEGS, 128), F32),
                ],
                axis=0,
            )
            column = jnp.where(iota((128, 128), 1) < 4, column, 0.0)
            out_ref[2 * k + tt, 4 * SEGS :, :] = spread3(column).T[:16].astype(BF16)
        return carry

    lax.fori_loop(0, KVH, step, 0, unroll=UNROLL)


def merge_kernel(target_ref, x_ref, keep_ref, give_ref, home_ref):
    lane = iota((8, 128), 1)
    lses = []
    for t in range(N_TP):
        parts = x_ref[t, 4 * SEGS :, :].astype(F32)
        lses.append(parts[0:4] + parts[4:8] + parts[8:12])
    lses = [jnp.concatenate([x, x], axis=0) for x in lses]
    for g in range(GROUPS + 1):
        halves = []
        for half in range(2):
            row = jnp.zeros((8, 128), F32)
            for j in range(8):
                shift = (16 * j - 16 * g) % 128
                moved = lses[half * 8 + j]
                moved = pltpu.roll(moved, shift, 1) if shift else moved
                row = jnp.where(jnp.right_shift(lane, 4) == j, moved, row)
            halves.append(row)
        lse = jnp.concatenate(halves, axis=1)
        high = 128 if g < GROUPS else ROWS
        rows = iota((high, 256), 0)
        if g < GROUPS:
            mask = rows.astype(F32) == target_ref[g, 0:1, :]
        else:
            mask = rows == jnp.bitwise_and(iota((high, 256), 1), 15)
        out_lse = jnp.zeros((high, 128), F32)
        out_lane = iota((high, 128), 1)
        mixed = []
        for h in range(4):
            at = h * SEGS + 16 * g
            values = x_ref[:, at : at + 16, :].reshape(256, HD)
            score = jnp.where(mask, lse[h : h + 1, :], DEAD)
            peak = jnp.max(score, axis=1, keepdims=True)
            weight = jnp.exp(score - peak)
            total = jnp.sum(weight, axis=1, keepdims=True)
            upper = weight.astype(BF16)
            lower = (weight - upper.astype(F32)).astype(BF16)
            both = dot(jnp.concatenate([upper, lower], axis=0), values)
            mixed.append((both[:high] + both[high:]) / total)
            out_lse = jnp.where(out_lane == h, peak + jnp.log(total), out_lse)
        mixed = jnp.concatenate(mixed + [out_lse], axis=1)
        if g < GROUPS:
            result = keep_ref if g < 2 else give_ref
            result[(g % 2) * 8 : (g % 2 + 1) * 8] = mixed.reshape(8, ROWS, WIDTH + 128)
        else:
            home_ref[...] = mixed


def join_kernel(keep_ref, come_ref, out_ref):
    for z in range(N_INST // 2):
        ours = keep_ref[z, :, WIDTH:]
        theirs = come_ref[z, :, WIDTH:]
        peak = jnp.maximum(ours, theirs)
        first = jnp.exp(ours - peak)
        second = jnp.exp(theirs - peak)
        total = first + second
        first = first / total
        second = second / total
        for h in range(4):
            cut = slice(h * HD, (h + 1) * HD)
            out_ref[z, :, cut] = (
                first[:, h : h + 1] * keep_ref[z, :, cut]
                + second[:, h : h + 1] * come_ref[z, :, cut]
            ).astype(BF16)
        lse = jnp.where(iota((ROWS, 128), 1) < 4, peak + jnp.log(total), 0.0)
        out_ref[z, :, WIDTH:] = spread3(lse).astype(BF16)


def final_kernel(home_ref, x_ref, out_ref):
    pieces = x_ref.shape[0]
    lses = [home_ref[:, WIDTH:]]
    for c in range(pieces):
        parts = x_ref[c, :, WIDTH:].astype(F32)
        lses.append(parts + pltpu.roll(parts, 124, 1) + pltpu.roll(parts, 120, 1))
    peak = functools.reduce(jnp.maximum, lses)
    weights = [jnp.exp(lse - peak) for lse in lses]
    total = sum(weights)
    for h in range(4):
        cut = slice(h * HD, (h + 1) * HD)
        mixed = weights[0][:, h : h + 1] * home_ref[:, cut]
        for c in range(pieces):
            mixed = mixed + weights[c + 1][:, h : h + 1] * x_ref[c, :, cut].astype(F32)
        out_ref[:, cut] = (mixed / total[:, h : h + 1]).astype(BF16)


VMEM = pl.BlockSpec(memory_space=pltpu.VMEM)
SMEM = pl.BlockSpec(memory_space=pltpu.SMEM)
PARAMS = pltpu.CompilerParams(vmem_limit_bytes=48 * 1024 * 1024)


def exchange(x, axis, groups=None):
    return lax.all_to_all(
        x, axis, split_axis=0, concat_axis=0, axis_index_groups=groups, tiled=True
    )


def call(kernel, name, out_shape, args, smem=0):
    specs = [SMEM] * smem + [VMEM] * (len(args) - smem)
    outs = jax.tree.map(lambda _: VMEM, out_shape)
    return pl.pallas_call(
        kernel,
        out_shape=out_shape,
        in_specs=specs,
        out_specs=outs,
        compiler_params=PARAMS,
        name=name,
    )(*args)


def per_device(
    queries,
    home_keys,
    home_values,
    home_table,
    home_len,
    lent_keys,
    lent_values,
    lend_row,
    lend_table,
    lend_len,
):
    chips = N_INST // 2
    same_core = [[2 * z + core for z in range(chips)] for core in range(2)]
    sibling = [(i, i ^ 1) for i in range(N_INST)]
    wide = WIDTH + 128
    me = lax.axis_index("inst").astype(jnp.int32)
    core = jnp.bitwise_and(me, 1)

    asked = exchange(jnp.broadcast_to(lend_row.reshape(1, SLOTS), (N_TP, SLOTS)), "tp")
    sent = jnp.concatenate(
        [queries, asked.astype(BF16), jnp.zeros((ROWS, 128 - SLOTS), BF16)], axis=1
    )
    mine = exchange(jnp.broadcast_to(sent[None], (chips, ROWS, wide)), "inst", same_core)
    other = lax.ppermute(mine, "inst", sibling)
    picked, target = call(
        pick_kernel,
        "pick",
        (
            jax.ShapeDtypeStruct((N_TP, SEGS, WIDTH), BF16),
            jax.ShapeDtypeStruct((GROUPS, 8, 256), F32),
        ),
        (me.reshape(1), mine, other),
        smem=1,
    )
    arrived = exchange(picked, "tp")

    meta = jnp.concatenate(
        [lend_table.reshape(chips, 2, 2, 2), lend_len.reshape(chips, 2, 2, 1)], axis=3
    )
    meta = jnp.stack([meta, meta[:, ::-1]])[core].transpose(3, 1, 0, 2).reshape(3, SLOTS)
    lent_meta = jnp.concatenate([meta, meta], axis=1)
    home_meta = jnp.concatenate([home_table.reshape(ROWS, 1), home_len], axis=1).T
    home_meta = jnp.pad(home_meta, ((0, 0), (0, 128 - ROWS)), constant_values=16)
    pools = call(
        prepare_kernel,
        "prepare",
        tuple(jax.ShapeDtypeStruct((KVH, n, 2 * HD), BF16) for n in (512, 512, 256, 256)),
        (lent_meta, home_meta, lent_keys, lent_values, home_keys, home_values),
    )
    partial = call(
        attend_kernel,
        "attend",
        jax.ShapeDtypeStruct((N_TP, 4 * SEGS + 16, HD), BF16),
        (arrived, *pools),
    )
    returned = exchange(partial, "tp")
    keep, give, home = call(
        merge_kernel,
        "merge",
        (
            jax.ShapeDtypeStruct((chips, ROWS, wide), F32),
            jax.ShapeDtypeStruct((chips, ROWS, wide), F32),
            jax.ShapeDtypeStruct((ROWS, wide), F32),
        ),
        (target, returned),
    )
    come = lax.ppermute(give, "inst", sibling)
    joined = call(
        join_kernel, "join", jax.ShapeDtypeStruct((chips, ROWS, wide), BF16), (keep, come)
    )
    back = exchange(joined, "inst", same_core)
    return call(
        final_kernel, "final", jax.ShapeDtypeStruct((ROWS, WIDTH), BF16), (home, back)
    )


def solution(mesh):
    in_specs = (
        P("inst", "tp"),
        P(("inst", "tp"), None, None),
        P(("inst", "tp"), None, None),
        P("inst", "tp", None),
        P("inst", "tp"),
        P(("inst", "tp"), None, None),
        P(("inst", "tp"), None, None),
        P("inst", None, "tp", None),
        P("inst", None, "tp", None, None),
        P("inst", None, "tp", None),
    )
    out_specs = P("inst", "tp")
    return jax.shard_map(
        per_device, mesh=mesh, in_specs=in_specs, out_specs=out_specs, check_vma=False
    )
```

```python
import functools
import math

import jax
import jax.numpy as jnp
import ml_dtypes
import numpy as np
from jax import lax
from jax.experimental import pallas as pl
from jax.experimental.pallas import tpu as pltpu
from jax.sharding import PartitionSpec as P

QH = 64
KVH = 8
HD = 128
N_INST = 32
N_TP = 16
ROWS = 16
SLOTS = 64
WIDTH = 512
CHIPS = N_INST // 2
HALF = SLOTS // 2
PIECE = 4 * HALF + 2 * ROWS + 16
DEAD = -1e30
SCALE = HD ** (-0.5)
F32 = jnp.float32
BF16 = jnp.bfloat16
FACTOR = SCALE * math.log2(math.e)
TWICE_HI = float(np.float32(1 / FACTOR).astype(ml_dtypes.bfloat16))
TWICE_LO = 1 / FACTOR - TWICE_HI
UNROLL = 8


def iota(shape, axis):
    return lax.broadcasted_iota(jnp.int32, shape, axis)


def dot(a, b):
    return jnp.dot(a, b, preferred_element_type=F32)


def dot_nt(a, b):
    return lax.dot_general(a, b, (((1,), (1,)), ((), ())), preferred_element_type=F32)


def split3(x):
    hi = x.astype(BF16).astype(F32)
    rest = x - hi
    mid = rest.astype(BF16).astype(F32)
    return hi, mid, rest - mid


def spread3(x):
    hi, mid, low = split3(x)
    return hi + pltpu.roll(mid, 4, 1) + pltpu.roll(low, 8, 1)


def spread_kernel(queries_ref, first_ref, out_ref):
    row = iota((ROWS, 128), 0)
    asked = jnp.zeros((ROWS, 128), F32)
    for t in range(N_TP):
        asked = jnp.where(row == t, first_ref[t, :, WIDTH:].astype(F32), asked)
    block = jnp.concatenate([queries_ref[...], asked.astype(BF16)], axis=1)
    for z in range(CHIPS):
        out_ref[z] = block


def pick_kernel(me_ref, mine_ref, out_ref, target_ref):
    chip = jnp.right_shift(me_ref[0], 1)
    k = iota((256, 128), 0)
    n = iota((256, 128), 1)
    local = jnp.bitwise_and(jnp.right_shift(k, 1), 7)
    order = jnp.where(n == local * 16 + jnp.right_shift(k, 4), 1.0, 0.0).astype(BF16)
    second = jnp.bitwise_and(k, 1) == 1
    base = local.astype(F32) * 16.0
    lane = n.astype(F32)
    row = iota((128, 128), 0)
    for g in range(2):
        block = mine_ref[g * 8 : (g + 1) * 8].reshape(128, WIDTH + 128)
        asked = dot(order, block[:, WIDTH:]).astype(BF16)
        for d in range(2):
            found = []
            for s in range(2):
                column = jnp.where(row == 4 * chip + 2 * d + s, 1.0, 0.0).astype(BF16)
                found.append(dot(asked, column))
            target = jnp.where(second, found[1], found[0]) + base
            onehot = jnp.where(lane == target, 1.0, 0.0).astype(BF16)
            picked = dot(onehot, block[:, :WIDTH]).astype(BF16)
            out_ref[d * N_TP : (d + 1) * N_TP, g * 16 : (g + 1) * 16, :] = picked.reshape(
                N_TP, 16, WIDTH
            )
            target_ref[g, :, d * 256 : (d + 1) * 256] = target.T[:8]


def prepare_kernel(
    lent_ref, home_ref, lk_ref, lv_ref, hk_ref, hv_ref, klent_ref, vlent_ref, khome_ref, vhome_ref
):
    token = iota((512, 128), 0)
    block = jnp.right_shift(token, 4)
    place = jnp.bitwise_and(token, 15)
    length = lent_ref[2:3, :]
    first = (block == lent_ref[0:1, :]) & (place < length)
    other = (block == lent_ref[1:2, :]) & (place + 16 < length)
    twice = first & other
    upper = jnp.where(first | other, jnp.where(twice, TWICE_HI, 0.0), DEAD)
    lower = jnp.where(twice, TWICE_LO, 0.0)
    lent_mask = jnp.where(iota((512, 128), 1) < SLOTS, upper, lower).astype(BF16)
    token = iota((256, 128), 0)
    live = (jnp.right_shift(token, 4) == home_ref[0:1, :]) & (
        jnp.bitwise_and(token, 15) < home_ref[1:2, :]
    )
    home_mask = jnp.where(live, 0.0, DEAD).astype(BF16)
    ones = jnp.ones((512, 128), BF16)
    for k in range(KVH):
        cut = slice(k * HD, (k + 1) * HD)
        klent_ref[k, :, :HD] = lk_ref[:, :, cut].reshape(512, HD)
        klent_ref[k, :, HD:] = lent_mask
        vlent_ref[k, :, :HD] = lv_ref[:, :, cut].reshape(512, HD)
        vlent_ref[k, :, HD:] = ones
        khome_ref[k, :, :HD] = hk_ref[:, :, cut].reshape(256, HD)
        khome_ref[k, :, HD:] = home_mask
        vhome_ref[k, :, :HD] = hv_ref[:, :, cut].reshape(256, HD)
        vhome_ref[k, :, HD:] = ones[:256]


def attend_kernel(x_ref, first_ref, klent_ref, vlent_ref, khome_ref, vhome_ref, out_ref):
    def pool(query, pick, keys, values, count):
        query = jnp.concatenate([query, jnp.concatenate([pick] * 8, axis=0)], axis=1)
        scores = dot_nt(query, keys)
        weights = []
        peaks = []
        for j in range(8):
            part = scores[j * count : (j + 1) * count]
            peak = jnp.max(part, axis=1, keepdims=True)
            weights.append(jnp.exp2((part - peak) * FACTOR).astype(BF16))
            peaks.append(peak)
        mixed = dot(jnp.concatenate(weights, axis=0), values)
        total = mixed[:, HD:]
        return (mixed[:, :HD] / total).astype(BF16), peaks, total

    def columns(tt, peaks, total, count):
        lane = iota((count, 128), 1)
        top = jnp.zeros((count, 128), F32)
        amount = jnp.ones((count, 128), F32)
        for h in range(4):
            j = tt * 4 + h
            top = jnp.where(lane == h, peaks[j], top)
            amount = jnp.where(lane == h, total[j * count : (j + 1) * count], amount)
        return jnp.where(top > DEAD / 2, top * SCALE + jnp.log(amount), DEAD)

    lane = iota((SLOTS, 128), 1)
    lent_pick = jnp.where(
        jnp.bitwise_and(lane, SLOTS - 1) == iota((SLOTS, 128), 0), 1.0, 0.0
    ).astype(BF16)
    home_pick = jnp.where(iota((ROWS, 128), 1) == iota((ROWS, 128), 0), 1.0, 0.0).astype(BF16)
    heads = [(tt, h) for tt in range(2) for h in range(4)]

    def step(k, carry):
        query = [
            x_ref[d * N_TP + 2 * k + tt, :, h * HD : (h + 1) * HD]
            for tt, h in heads
            for d in range(2)
        ]
        lent, lent_peaks, lent_total = pool(
            jnp.concatenate(query, axis=0), lent_pick, klent_ref[k], vlent_ref[k], SLOTS
        )
        query = [first_ref[2 * k + tt, :, h * HD : (h + 1) * HD] for tt, h in heads]
        home, home_peaks, home_total = pool(
            jnp.concatenate(query, axis=0), home_pick, khome_ref[k], vhome_ref[k], ROWS
        )
        for tt in range(2):
            lent_lse = columns(tt, lent_peaks, lent_total, SLOTS)
            home_lse = columns(tt, home_peaks, home_total, ROWS)
            rest = jnp.zeros((ROWS, 128), F32)
            column = jnp.concatenate(
                [lent_lse[:HALF], home_lse, rest, lent_lse[HALF:], home_lse, rest], axis=0
            )
            column = jnp.where(iota((128, 128), 1) < 4, column, 0.0)
            lse = spread3(column).T[:16]
            for d in range(2):
                to = d * N_TP + 2 * k + tt
                for h in range(4):
                    at = (tt * 4 + h) * SLOTS + d * HALF
                    out_ref[to, h * HALF : (h + 1) * HALF, :] = lent[at : at + HALF]
                for hh in range(2):
                    at = (tt * 4 + 2 * d + hh) * ROWS
                    to_row = 4 * HALF + hh * ROWS
                    out_ref[to, to_row : to_row + ROWS, :] = home[at : at + ROWS]
                out_ref[to, PIECE - 16 :, :] = (pltpu.roll(lse, 64, 1) if d else lse).astype(BF16)
        return carry

    lax.fori_loop(0, KVH, step, 0, unroll=UNROLL)


def merge_kernel(me_ref, target_ref, x_ref, out_ref, keep_ref, give_ref):
    core = jnp.bitwise_and(me_ref[0], 1)
    lane = iota((8, 128), 1)
    lses = []
    for t in range(2 * N_TP):
        parts = x_ref[t, PIECE - 16 :, :].astype(F32)
        lses.append(parts[0:4] + parts[4:8] + parts[8:12])
    lses = [jnp.concatenate([x, x], axis=0) for x in lses]

    def gather(sources, first):
        chunks = []
        for at in range(0, len(sources), 8):
            row = jnp.zeros((8, 128), F32)
            for j in range(8):
                shift = (16 * j - first) % 128
                moved = lses[sources[at + j]]
                moved = pltpu.roll(moved, shift, 1) if shift else moved
                row = jnp.where(jnp.right_shift(lane, 4) == j, moved, row)
            chunks.append(row)
        return jnp.concatenate(chunks, axis=1)

    def join(mask, lse, values):
        score = jnp.where(mask, lse, DEAD)
        peak = jnp.max(score, axis=1, keepdims=True)
        weight = jnp.exp(score - peak)
        total = jnp.sum(weight, axis=1, keepdims=True)
        upper = weight.astype(BF16)
        lower = (weight - upper.astype(F32)).astype(BF16)
        both = dot(jnp.concatenate([upper, lower], axis=0), values)
        count = mask.shape[0]
        return (both[:count] + both[count:]) / total, peak + jnp.log(total)

    rows = iota((128, 512), 0).astype(F32)
    out_lane = iota((128, 128), 1)
    for g in range(2):
        lse = gather(list(range(2 * N_TP)), 16 * g)
        mask = rows == target_ref[g, 0:1, :]
        out_lse = jnp.zeros((128, 128), F32)
        block = slice(g * 8, (g + 1) * 8)
        for h in range(4):
            at = h * HALF + 16 * g
            values = x_ref[:, at : at + 16, :].reshape(512, HD)
            mixed, total = join(mask, lse[h : h + 1, :], values)
            out_lse = jnp.where(out_lane == h, total, out_lse)
            out_ref[block, :, h * HD : (h + 1) * HD] = mixed.astype(BF16).reshape(8, ROWS, HD)
        out_ref[block, :, WIDTH:] = spread3(out_lse).astype(BF16).reshape(8, ROWS, 128)
    mask = iota((ROWS, 256), 0) == jnp.bitwise_and(iota((ROWS, 256), 1), 15)
    home_lane = iota((ROWS, 128), 1)
    homes = []
    for d in range(2):
        lse = gather(list(range(d * N_TP, (d + 1) * N_TP)), HALF)
        lse = jnp.where(core == 0, lse[0:2], lse[2:4])
        out_lse = jnp.zeros((ROWS, 128), F32)
        parts = []
        for hh in range(2):
            at = 4 * HALF + hh * ROWS
            values = x_ref[d * N_TP : (d + 1) * N_TP, at : at + ROWS, :].reshape(256, HD)
            mixed, total = join(mask, lse[hh : hh + 1, :], values)
            parts.append(mixed)
            out_lse = jnp.where(home_lane == hh, total, out_lse)
        homes.append(jnp.concatenate(parts + [out_lse], axis=1))
    keep_ref[...] = jnp.where(core == 0, homes[0], homes[1])
    give_ref[...] = jnp.where(core == 0, homes[1], homes[0])


def final_kernel(me_ref, keep_ref, come_ref, x_ref, out_ref):
    core = jnp.bitwise_and(me_ref[0], 1)
    low = jnp.where(core == 0, keep_ref[...], come_ref[...])
    high = jnp.where(core == 0, come_ref[...], keep_ref[...])
    lane = iota((ROWS, 128), 1)
    lses = [jnp.where(lane < 2, low[:, 2 * HD :], pltpu.roll(high[:, 2 * HD :], 2, 1))]
    for c in range(CHIPS):
        parts = x_ref[c, :, WIDTH:].astype(F32)
        lses.append(parts + pltpu.roll(parts, 124, 1) + pltpu.roll(parts, 120, 1))
    peak = functools.reduce(jnp.maximum, lses)
    weights = [jnp.exp(lse - peak) for lse in lses]
    total = sum(weights)
    for h in range(4):
        cut = slice(h * HD, (h + 1) * HD)
        home = (low if h < 2 else high)[:, (h % 2) * HD : (h % 2 + 1) * HD]
        mixed = weights[0][:, h : h + 1] * home
        for c in range(CHIPS):
            mixed = mixed + weights[c + 1][:, h : h + 1] * x_ref[c, :, cut].astype(F32)
        out_ref[:, cut] = (mixed / total[:, h : h + 1]).astype(BF16)


VMEM = pl.BlockSpec(memory_space=pltpu.VMEM)
SMEM = pl.BlockSpec(memory_space=pltpu.SMEM)
PARAMS = pltpu.CompilerParams(vmem_limit_bytes=24 * 1024 * 1024)


def exchange(x, axis, groups=None):
    return lax.all_to_all(
        x, axis, split_axis=0, concat_axis=0, axis_index_groups=groups, tiled=True
    )


def call(kernel, name, out_shape, args, smem=0):
    specs = [SMEM] * smem + [VMEM] * (len(args) - smem)
    outs = jax.tree.map(lambda _: VMEM, out_shape)
    return pl.pallas_call(
        kernel,
        out_shape=out_shape,
        in_specs=specs,
        out_specs=outs,
        compiler_params=PARAMS,
        name=name,
    )(*args)


def per_device(
    queries,
    home_keys,
    home_values,
    home_table,
    home_len,
    lent_keys,
    lent_values,
    lend_row,
    lend_table,
    lend_len,
):
    same_core = [[2 * z + core for z in range(CHIPS)] for core in range(2)]
    plane = [[(2 * z) * N_TP + j for j in range(2 * N_TP)] for z in range(CHIPS)]
    sibling = [(i, i ^ 1) for i in range(N_INST)]
    wide = WIDTH + 128
    me = lax.axis_index("inst").astype(jnp.int32).reshape(1)

    asked = jnp.broadcast_to(lend_row.reshape(1, SLOTS).astype(BF16), (ROWS, SLOTS))
    asked = jnp.pad(asked, ((0, 0), (0, 128 - SLOTS)))
    sent = jnp.concatenate([queries, asked], axis=1)
    first = exchange(jnp.broadcast_to(sent[None], (N_TP, ROWS, wide)), "tp")
    sent = call(
        spread_kernel, "spread", jax.ShapeDtypeStruct((CHIPS, ROWS, wide), BF16), (queries, first)
    )
    mine = exchange(sent, "inst", same_core)
    picked, target = call(
        pick_kernel,
        "pick",
        (
            jax.ShapeDtypeStruct((2 * N_TP, HALF, WIDTH), BF16),
            jax.ShapeDtypeStruct((2, 8, 512), F32),
        ),
        (me, mine),
        smem=1,
    )
    arrived = exchange(picked, ("inst", "tp"), plane)

    meta = jnp.concatenate(
        [lend_table.reshape(CHIPS, 2, 2, 2), lend_len.reshape(CHIPS, 2, 2, 1)], axis=3
    )
    meta = meta.transpose(3, 1, 0, 2).reshape(3, SLOTS)
    lent_meta = jnp.concatenate([meta, meta], axis=1)
    home_meta = jnp.concatenate([home_table.reshape(ROWS, 1), home_len], axis=1).T
    home_meta = jnp.pad(home_meta, ((0, 0), (0, 128 - ROWS)), constant_values=16)
    pools = call(
        prepare_kernel,
        "prepare",
        tuple(jax.ShapeDtypeStruct((KVH, n, 2 * HD), BF16) for n in (512, 512, 256, 256)),
        (lent_meta, home_meta, lent_keys, lent_values, home_keys, home_values),
    )
    partial = call(
        attend_kernel,
        "attend",
        jax.ShapeDtypeStruct((2 * N_TP, PIECE, HD), BF16),
        (arrived, first, *pools),
    )
    returned = exchange(partial, ("inst", "tp"), plane)
    merged, keep, give = call(
        merge_kernel,
        "merge",
        (
            jax.ShapeDtypeStruct((CHIPS, ROWS, wide), BF16),
            jax.ShapeDtypeStruct((ROWS, 3 * HD), F32),
            jax.ShapeDtypeStruct((ROWS, 3 * HD), F32),
        ),
        (me, target, returned),
        smem=1,
    )
    come = lax.ppermute(give, "inst", sibling)
    back = exchange(merged, "inst", same_core)
    return call(
        final_kernel,
        "final",
        jax.ShapeDtypeStruct((ROWS, WIDTH), BF16),
        (me, keep, come, back),
        smem=1,
    )


def solution(mesh):
    in_specs = (
        P("inst", "tp"),
        P(("inst", "tp"), None, None),
        P(("inst", "tp"), None, None),
        P("inst", "tp", None),
        P("inst", "tp"),
        P(("inst", "tp"), None, None),
        P(("inst", "tp"), None, None),
        P("inst", None, "tp", None),
        P("inst", None, "tp", None, None),
        P("inst", None, "tp", None),
    )
    out_specs = P("inst", "tp")
    return jax.shard_map(
        per_device, mesh=mesh, in_specs=in_specs, out_specs=out_specs, check_vma=False
    )
```

```python
import functools
import math

import jax
import jax.numpy as jnp
import ml_dtypes
import numpy as np
from jax import lax
from jax.experimental import pallas as pl
from jax.experimental.pallas import tpu as pltpu
from jax.sharding import PartitionSpec as P

QH = 64
KVH = 8
HD = 128
N_INST = 32
N_TP = 16
ROWS = 16
SLOTS = 64
WIDTH = 512
CHIPS = N_INST // 2
HALF = SLOTS // 2
PIECE = 4 * HALF + 2 * ROWS + 16
DEAD = -1e30
SCALE = HD ** (-0.5)
F32 = jnp.float32
BF16 = jnp.bfloat16
FACTOR = SCALE * math.log2(math.e)
TWICE_HI = float(np.float32(1 / FACTOR).astype(ml_dtypes.bfloat16))
TWICE_LO = 1 / FACTOR - TWICE_HI


def iota(shape, axis):
    return lax.broadcasted_iota(jnp.int32, shape, axis)


def dot(a, b):
    return jnp.dot(a, b, preferred_element_type=F32)


def dot_nt(a, b):
    return lax.dot_general(a, b, (((1,), (1,)), ((), ())), preferred_element_type=F32)


def split3(x):
    hi = x.astype(BF16).astype(F32)
    rest = x - hi
    mid = rest.astype(BF16).astype(F32)
    return hi, mid, rest - mid


def spread3(x):
    hi, mid, low = split3(x)
    return hi + pltpu.roll(mid, 4, 1) + pltpu.roll(low, 8, 1)


def turn(x, by):
    return pltpu.roll(x, by % 128, 1) if by % 128 else x


def head_rows(h):
    return slice(h * ROWS, (h + 1) * ROWS)


def open_kernel(lend_ref, queries_ref, out_ref, lend_s):
    lend_s[...] = jnp.zeros_like(lend_s)
    lend_s[0:2, 0:N_INST] = lend_ref[...]
    lend = lend_s[...].astype(F32).astype(BF16)
    for t in range(N_TP):
        for h in range(4):
            out_ref[t, head_rows(h), :] = queries_ref[:, h * HD : (h + 1) * HD]
        out_ref[t, 4 * ROWS :, :] = lend


def spread_kernel(me_ref, first_ref, out_ref):
    row = iota((8, 128), 0)
    asked = jnp.zeros((8, 128), F32)
    for t in range(N_TP):
        part = first_ref[t, 4 * ROWS :, :].astype(F32)
        place = 64 * (t // 8)
        line = turn(part, place)[0:1] + turn(part, place + 32)[1:2]
        asked = asked + jnp.where(row == t % 8, line, 0.0)
    asked = asked.astype(BF16)
    queries = first_ref[me_ref[1], : 4 * ROWS, :]
    for z in range(CHIPS):
        out_ref[z, : 4 * ROWS, :] = queries
        out_ref[z, 4 * ROWS :, :] = asked


def places(me, mine_ref, g, d):
    k = iota((256, 64), 0)
    local = jnp.bitwise_and(jnp.right_shift(k, 1), 7)
    source = local * 8 + jnp.bitwise_and(jnp.right_shift(k, 4), 7)
    order = jnp.where(iota((256, 64), 1) == source, 1.0, 0.0).astype(BF16)
    asked = mine_ref[g * 8 : (g + 1) * 8, 4 * ROWS :, :].astype(F32).reshape(64, 128)
    asked = dot(order, asked.astype(BF16))
    k = iota((256, 128), 0)
    creditor = 2 * jnp.right_shift(me, 1) + d
    column = jnp.right_shift(k, 7) * 64 + jnp.bitwise_and(k, 1) * 32 + creditor
    asked = jnp.where(iota((256, 128), 1) == column, asked, 0.0).astype(BF16)
    local = jnp.bitwise_and(jnp.right_shift(k, 1), 7)
    return dot(asked, jnp.ones((128, 128), BF16)) + local.astype(F32) * 16.0


def pick_kernel(me_ref, mine_ref, out_ref):
    lane = iota((256, 128), 1).astype(F32)
    for g in range(2):
        block = jnp.concatenate(
            [
                mine_ref[g * 8 : (g + 1) * 8, head_rows(h), :].reshape(128, HD)
                for h in range(4)
            ],
            axis=1,
        )
        for d in range(2):
            target = places(me_ref[0], mine_ref, g, d)
            onehot = jnp.where(lane == target, 1.0, 0.0).astype(BF16)
            picked = dot(onehot, block).astype(BF16)
            out_ref[d * N_TP : (d + 1) * N_TP, g * 16 : (g + 1) * 16, :] = picked.reshape(
                N_TP, 16, WIDTH
            )


def places_kernel(me_ref, mine_ref, out_ref):
    for g in range(2):
        for d in range(2):
            target = places(me_ref[0], mine_ref, g, d)
            out_ref[g, :, d * 256 : (d + 1) * 256] = target.T[:8]


def masks_kernel(lent_ref, home_ref, lent_out, home_out):
    token = iota((512, 128), 0)
    block = jnp.right_shift(token, 4)
    place = jnp.bitwise_and(token, 15)
    length = lent_ref[2:3, :]
    first = (block == lent_ref[0:1, :]) & (place < length)
    other = (block == lent_ref[1:2, :]) & (place + 16 < length)
    twice = first & other
    upper = jnp.where(first | other, jnp.where(twice, TWICE_HI, 0.0), DEAD)
    lower = jnp.where(twice, TWICE_LO, 0.0)
    lent_out[...] = jnp.where(iota((512, 128), 1) < SLOTS, upper, lower).astype(BF16)
    token = iota((256, 128), 0)
    live = (jnp.right_shift(token, 4) == home_ref[0:1, :]) & (
        jnp.bitwise_and(token, 15) < home_ref[1:2, :]
    )
    home_out[...] = jnp.where(live, 0.0, DEAD).astype(BF16)


def attend_kernel(
    x_ref,
    first_ref,
    lent_mask_ref,
    home_mask_ref,
    lk_ref,
    lv_ref,
    hk_ref,
    hv_ref,
    out_ref,
    lk_s,
    lv_s,
    hk_s,
    hv_s,
    sems,
):
    def fetch(k):
        cut = slice(k * HD, (k + 1) * HD)
        pairs = ((lk_ref, lk_s), (lv_ref, lv_s), (hk_ref, hk_s), (hv_ref, hv_s))
        return [
            pltpu.make_async_copy(source.at[:, :, cut], to.at[k], sems.at[k, j])
            for j, (source, to) in enumerate(pairs)
        ]

    copies = [fetch(k) for k in range(KVH)]
    for group in copies:
        for copy in group:
            copy.start()

    def pool(query, pick, keys, values, count):
        query = jnp.concatenate([query, jnp.concatenate([pick] * 8, axis=0)], axis=1)
        scores = dot_nt(query, keys)
        weights = []
        peaks = []
        for j in range(8):
            part = scores[j * count : (j + 1) * count]
            peak = jnp.max(part, axis=1, keepdims=True)
            weights.append(jnp.exp2((part - peak) * FACTOR).astype(BF16))
            peaks.append(peak)
        mixed = dot(jnp.concatenate(weights, axis=0), values)
        total = mixed[:, HD:]
        return (mixed[:, :HD] / total).astype(BF16), peaks, total

    def columns(tt, peaks, total, count):
        lane = iota((count, 128), 1)
        top = jnp.zeros((count, 128), F32)
        amount = jnp.ones((count, 128), F32)
        for h in range(4):
            j = tt * 4 + h
            top = jnp.where(lane == h, peaks[j], top)
            amount = jnp.where(lane == h, total[j * count : (j + 1) * count], amount)
        return jnp.where(top > DEAD / 2, top * SCALE + jnp.log(amount), DEAD)

    lane = iota((SLOTS, 128), 1)
    lent_pick = jnp.where(
        jnp.bitwise_and(lane, SLOTS - 1) == iota((SLOTS, 128), 0), 1.0, 0.0
    ).astype(BF16)
    home_pick = jnp.where(iota((ROWS, 128), 1) == iota((ROWS, 128), 0), 1.0, 0.0).astype(BF16)
    heads = [(tt, h) for tt in range(2) for h in range(4)]

    lent_mask = lent_mask_ref[...]
    home_mask = home_mask_ref[...]
    ones = jnp.ones((512, 128), BF16)
    for k in range(KVH):
        for copy in copies[k]:
            copy.wait()
        lent_k = jnp.concatenate([lk_s[k].reshape(512, HD), lent_mask], axis=1)
        lent_v = jnp.concatenate([lv_s[k].reshape(512, HD), ones], axis=1)
        home_k = jnp.concatenate([hk_s[k].reshape(256, HD), home_mask], axis=1)
        home_v = jnp.concatenate([hv_s[k].reshape(256, HD), ones[:256]], axis=1)
        query = [
            x_ref[d * N_TP + 2 * k + tt, :, h * HD : (h + 1) * HD]
            for tt, h in heads
            for d in range(2)
        ]
        lent, lent_peaks, lent_total = pool(
            jnp.concatenate(query, axis=0), lent_pick, lent_k, lent_v, SLOTS
        )
        query = [first_ref[2 * k + tt, head_rows(h), :] for tt, h in heads]
        home, home_peaks, home_total = pool(
            jnp.concatenate(query, axis=0), home_pick, home_k, home_v, ROWS
        )
        for tt in range(2):
            lent_lse = columns(tt, lent_peaks, lent_total, SLOTS)
            home_lse = columns(tt, home_peaks, home_total, ROWS)
            rest = jnp.zeros((ROWS, 128), F32)
            column = jnp.concatenate(
                [lent_lse[:HALF], home_lse, rest, lent_lse[HALF:], home_lse, rest], axis=0
            )
            column = jnp.where(iota((128, 128), 1) < 4, column, 0.0)
            lse = spread3(column).T[:16]
            for d in range(2):
                to = d * N_TP + 2 * k + tt
                for h in range(4):
                    at = (tt * 4 + h) * SLOTS + d * HALF
                    out_ref[to, h * HALF : (h + 1) * HALF, :] = lent[at : at + HALF]
                for hh in range(2):
                    at = (tt * 4 + 2 * d + hh) * ROWS
                    to_row = 4 * HALF + hh * ROWS
                    out_ref[to, to_row : to_row + ROWS, :] = home[at : at + ROWS]
                out_ref[to, PIECE - 16 :, :] = (pltpu.roll(lse, 64, 1) if d else lse).astype(BF16)


def merge_kernel(me_ref, target_ref, x_ref, out_ref, keep_ref, give_ref):
    core = jnp.bitwise_and(me_ref[0], 1)
    lane = iota((8, 128), 1)
    lses = []
    for t in range(2 * N_TP):
        parts = x_ref[t, PIECE - 16 :, :].astype(F32)
        lses.append(parts[0:4] + parts[4:8] + parts[8:12])
    lses = [jnp.concatenate([x, x], axis=0) for x in lses]

    def gather(sources, first):
        chunks = []
        for at in range(0, len(sources), 8):
            row = jnp.zeros((8, 128), F32)
            for j in range(8):
                moved = turn(lses[sources[at + j]], 16 * j - first)
                row = jnp.where(jnp.right_shift(lane, 4) == j, moved, row)
            chunks.append(row)
        return jnp.concatenate(chunks, axis=1)

    def join(mask, lse, values):
        score = jnp.where(mask, lse, DEAD)
        peak = jnp.max(score, axis=1, keepdims=True)
        weight = jnp.exp(score - peak)
        total = jnp.sum(weight, axis=1, keepdims=True)
        upper = weight.astype(BF16)
        lower = (weight - upper.astype(F32)).astype(BF16)
        both = dot(jnp.concatenate([upper, lower], axis=0), values)
        count = mask.shape[0]
        return (both[:count] + both[count:]) / total, peak + jnp.log(total)

    rows = iota((128, 512), 0).astype(F32)
    out_lane = iota((128, 128), 1)
    for g in range(2):
        lse = gather(list(range(2 * N_TP)), 16 * g)
        mask = rows == target_ref[g, 0:1, :]
        out_lse = jnp.zeros((128, 128), F32)
        block = slice(g * 8, (g + 1) * 8)
        for h in range(4):
            at = h * HALF + 16 * g
            values = x_ref[:, at : at + 16, :].reshape(512, HD)
            mixed, total = join(mask, lse[h : h + 1, :], values)
            out_lse = jnp.where(out_lane == h, total, out_lse)
            out_ref[block, head_rows(h), :] = mixed.astype(BF16).reshape(8, ROWS, HD)
        hi, mid, low = split3(out_lse.T[:8])
        for j in range(8):
            line = jnp.where(lane < 32, turn(mid, 16 - 16 * j), 0.0)
            line = jnp.where(lane < 16, turn(hi, -16 * j), line)
            line = jnp.where(
                (lane >= 32) & (lane < 48), turn(low, 32 - 16 * j), line
            )
            out_ref[g * 8 + j, 4 * ROWS :, :] = line.astype(BF16)
    mask = iota((ROWS, 256), 0) == jnp.bitwise_and(iota((ROWS, 256), 1), 15)
    home_lane = iota((ROWS, 128), 1)
    homes = []
    for d in range(2):
        lse = gather(list(range(d * N_TP, (d + 1) * N_TP)), HALF)
        lse = jnp.where(core == 0, lse[0:2], lse[2:4])
        out_lse = jnp.zeros((ROWS, 128), F32)
        parts = []
        for hh in range(2):
            at = 4 * HALF + hh * ROWS
            values = x_ref[d * N_TP : (d + 1) * N_TP, at : at + ROWS, :].reshape(256, HD)
            mixed, total = join(mask, lse[hh : hh + 1, :], values)
            parts.append(mixed)
            out_lse = jnp.where(home_lane == hh, total, out_lse)
        homes.append(jnp.concatenate(parts + [out_lse], axis=1))
    keep_ref[...] = jnp.where(core == 0, homes[0], homes[1])
    give_ref[...] = jnp.where(core == 0, homes[1], homes[0])


def final_kernel(me_ref, keep_ref, come_ref, x_ref, out_ref):
    core = jnp.bitwise_and(me_ref[0], 1)
    low = jnp.where(core == 0, keep_ref[...], come_ref[...])
    high = jnp.where(core == 0, come_ref[...], keep_ref[...])
    lane = iota((ROWS, 128), 1)
    lse = jnp.where(lane < 2, low[:, 2 * HD :], pltpu.roll(high[:, 2 * HD :], 2, 1))
    lses = [jnp.concatenate([lse, jnp.zeros((128 - ROWS, 128), F32)], axis=0).T[:8]]
    for c in range(CHIPS):
        parts = x_ref[c, 4 * ROWS :, :].astype(F32)
        lses.append(parts + turn(parts, -16) + turn(parts, -32))
    peak = functools.reduce(jnp.maximum, lses)
    weights = [jnp.exp(lse - peak) for lse in lses]
    total = sum(weights)
    weights = [weight / total for weight in weights]
    home_weight = jnp.concatenate([weights[0], jnp.zeros((120, 128), F32)], axis=0).T[:ROWS]
    lent_weight = jnp.concatenate(weights[1:], axis=0).T[:ROWS]
    for h in range(4):
        home = (low if h < 2 else high)[:, (h % 2) * HD : (h % 2 + 1) * HD]
        mixed = home_weight[:, h : h + 1] * home
        for c in range(CHIPS):
            at = c * 8 + h
            mixed = mixed + lent_weight[:, at : at + 1] * x_ref[c, head_rows(h), :].astype(F32)
        out_ref[:, h * HD : (h + 1) * HD] = mixed.astype(BF16)


VMEM = pl.BlockSpec(memory_space=pltpu.VMEM)
SMEM = pl.BlockSpec(memory_space=pltpu.SMEM)
ANY = pl.BlockSpec(memory_space=pl.ANY)
PARAMS = pltpu.CompilerParams(vmem_limit_bytes=24 * 1024 * 1024)


def exchange(x, axis, groups=None):
    return lax.all_to_all(
        x, axis, split_axis=0, concat_axis=0, axis_index_groups=groups, tiled=True
    )


def call(kernel, name, out_shape, args, smem=0, any_last=0, scratch=()):
    specs = [SMEM] * smem + [VMEM] * (len(args) - smem - any_last) + [ANY] * any_last
    return pl.pallas_call(
        kernel,
        out_shape=out_shape,
        in_specs=specs,
        out_specs=jax.tree.map(lambda _: VMEM, out_shape),
        scratch_shapes=scratch,
        compiler_params=PARAMS,
        name=name,
    )(*args)


def per_device(
    queries,
    home_keys,
    home_values,
    home_table,
    home_len,
    lent_keys,
    lent_values,
    lend_row,
    lend_table,
    lend_len,
):
    same_core = [[2 * z + core for z in range(CHIPS)] for core in range(2)]
    plane = [[(2 * z) * N_TP + j for j in range(2 * N_TP)] for z in range(CHIPS)]
    sibling = [(i, i ^ 1) for i in range(N_INST)]
    block = (CHIPS, 4 * ROWS + 8, HD)
    me = jnp.stack([lax.axis_index("inst"), lax.axis_index("tp")]).astype(jnp.int32)

    sent = call(
        open_kernel,
        "open",
        jax.ShapeDtypeStruct(block, BF16),
        (lend_row.reshape(N_INST, 2).T, queries),
        scratch=(pltpu.VMEM((8, 128), jnp.int32),),
    )
    first = exchange(sent, "tp")
    sent = call(spread_kernel, "spread", jax.ShapeDtypeStruct(block, BF16), (me, first), smem=1)
    mine = exchange(sent, "inst", same_core)
    picked = call(
        pick_kernel,
        "pick",
        jax.ShapeDtypeStruct((2 * N_TP, HALF, WIDTH), BF16),
        (me, mine),
        smem=1,
    )
    arrived = exchange(picked, ("inst", "tp"), plane)
    target = call(
        places_kernel, "places", jax.ShapeDtypeStruct((2, 8, 512), F32), (me, mine), smem=1
    )

    meta = jnp.concatenate(
        [lend_table.reshape(CHIPS, 2, 2, 2), lend_len.reshape(CHIPS, 2, 2, 1)], axis=3
    )
    meta = meta.transpose(3, 1, 0, 2).reshape(3, SLOTS)
    lent_meta = jnp.concatenate([meta, meta], axis=1)
    home_meta = jnp.concatenate([home_table.reshape(ROWS, 1), home_len], axis=1).T
    home_meta = jnp.pad(home_meta, ((0, 0), (0, 128 - ROWS)), constant_values=16)
    masks = call(
        masks_kernel,
        "masks",
        (jax.ShapeDtypeStruct((512, 128), BF16), jax.ShapeDtypeStruct((256, 128), BF16)),
        (lent_meta, home_meta),
    )
    partial = call(
        attend_kernel,
        "attend",
        jax.ShapeDtypeStruct((2 * N_TP, PIECE, HD), BF16),
        (arrived, first, *masks, lent_keys, lent_values, home_keys, home_values),
        any_last=4,
        scratch=(
            pltpu.VMEM((KVH, 32, 16, HD), BF16),
            pltpu.VMEM((KVH, 32, 16, HD), BF16),
            pltpu.VMEM((KVH, 16, 16, HD), BF16),
            pltpu.VMEM((KVH, 16, 16, HD), BF16),
            pltpu.SemaphoreType.DMA((KVH, 4)),
        ),
    )
    returned = exchange(partial, ("inst", "tp"), plane)
    merged, keep, give = call(
        merge_kernel,
        "merge",
        (
            jax.ShapeDtypeStruct(block, BF16),
            jax.ShapeDtypeStruct((ROWS, 3 * HD), F32),
            jax.ShapeDtypeStruct((ROWS, 3 * HD), F32),
        ),
        (me, target, returned),
        smem=1,
    )
    come = lax.ppermute(give, "inst", sibling)
    back = exchange(merged, "inst", same_core)
    return call(
        final_kernel,
        "final",
        jax.ShapeDtypeStruct((ROWS, WIDTH), BF16),
        (me, keep, come, back),
        smem=1,
    )


def solution(mesh):
    in_specs = (
        P("inst", "tp"),
        P(("inst", "tp"), None, None),
        P(("inst", "tp"), None, None),
        P("inst", "tp", None),
        P("inst", "tp"),
        P(("inst", "tp"), None, None),
        P(("inst", "tp"), None, None),
        P("inst", None, "tp", None),
        P("inst", None, "tp", None, None),
        P("inst", None, "tp", None),
    )
    out_specs = P("inst", "tp")
    return jax.shard_map(
        per_device, mesh=mesh, in_specs=in_specs, out_specs=out_specs, check_vma=False
    )
```

```python
import functools
import math

import jax
import jax.numpy as jnp
import ml_dtypes
import numpy as np
from jax import lax
from jax.experimental import pallas as pl
from jax.experimental.pallas import tpu as pltpu
from jax.sharding import PartitionSpec as P

QH = 64
KVH = 8
HD = 128
N_INST = 32
N_TP = 16
ROWS = 16
SLOTS = 64
WIDTH = 512
CHIPS = N_INST // 2
HALF = SLOTS // 2
PIECE = 4 * HALF + 2 * ROWS + 16
DEAD = -1e30
SCALE = HD ** (-0.5)
F32 = jnp.float32
BF16 = jnp.bfloat16
FACTOR = SCALE * math.log2(math.e)
TWICE_HI = float(np.float32(1 / FACTOR).astype(ml_dtypes.bfloat16))
TWICE_LO = 1 / FACTOR - TWICE_HI


def iota(shape, axis):
    return lax.broadcasted_iota(jnp.int32, shape, axis)


def dot(a, b):
    return jnp.dot(a, b, preferred_element_type=F32)


def dot_nt(a, b):
    return lax.dot_general(a, b, (((1,), (1,)), ((), ())), preferred_element_type=F32)


def split3(x):
    hi = x.astype(BF16).astype(F32)
    rest = x - hi
    mid = rest.astype(BF16).astype(F32)
    return hi, mid, rest - mid


def spread3(x):
    hi, mid, low = split3(x)
    return hi + pltpu.roll(mid, 4, 1) + pltpu.roll(low, 8, 1)


def turn(x, by):
    return pltpu.roll(x, by % 128, 1) if by % 128 else x


def head_rows(h):
    return slice(h * ROWS, (h + 1) * ROWS)


def fold(x):
    lane = iota(x[..., :8, :].shape, x.ndim - 1)
    return jnp.where(lane < 64, x[..., :8, :], pltpu.roll(x[..., 8:, :], 64, x.ndim - 1))


def unfold(x):
    return jnp.concatenate([x, pltpu.roll(x, 64, x.ndim - 1)], axis=x.ndim - 2)


def spread_kernel(me_ref, first_ref, out_ref):
    row = iota((8, 128), 0)
    asked = jnp.zeros((8, 128), F32)
    for t in range(N_TP):
        part = first_ref[t, :, WIDTH:].astype(F32)
        line = turn(part[:8] + turn(part[8:], N_INST), 64 * (t // 8))
        asked = asked + jnp.where(row == t % 8, line, 0.0)
    asked = asked.astype(BF16)
    queries = first_ref[me_ref[1], :, :WIDTH]
    for z in range(CHIPS):
        for h in range(4):
            out_ref[z, head_rows(h), :] = queries[:, h * HD : (h + 1) * HD]
        out_ref[z, 4 * ROWS :, :] = asked


def places(me, mine_ref, g):
    k = iota((256, 128), 0)
    n = iota((256, 128), 1)
    local = jnp.bitwise_and(jnp.right_shift(k, 1), 7)
    order = jnp.where(n == local * 16 + jnp.right_shift(k, 4), 1.0, 0.0).astype(BF16)
    asked = mine_ref[g * 8 : (g + 1) * 8, 4 * ROWS :, :].astype(F32)
    asked = dot(order, unfold(asked).reshape(128, 128).astype(BF16))
    column = 2 * jnp.right_shift(me, 1) + N_INST * jnp.bitwise_and(k, 1)
    ones = jnp.ones((128, 128), BF16)
    base = local.astype(F32) * 16.0
    return [
        dot(jnp.where(n == column + d, asked, 0.0).astype(BF16), ones) + base
        for d in range(2)
    ]


def pick_kernel(me_ref, mine_ref, out_ref, target_ref):
    lane = iota((256, 128), 1).astype(F32)
    for g in range(2):
        block = jnp.concatenate(
            [
                mine_ref[g * 8 : (g + 1) * 8, head_rows(h), :].reshape(128, HD)
                for h in range(4)
            ],
            axis=1,
        )
        for d, target in enumerate(places(me_ref[0], mine_ref, g)):
            onehot = jnp.where(lane == target, 1.0, 0.0).astype(BF16)
            picked = dot(onehot, block).astype(BF16)
            out_ref[d * N_TP : (d + 1) * N_TP, g * 16 : (g + 1) * 16, :] = picked.reshape(
                N_TP, 16, WIDTH
            )
            target_ref[g, :, d * 256 : (d + 1) * 256] = target.T[:8]


def masks_kernel(lent_ref, out_ref):
    token = iota((512, 128), 0)
    block = jnp.right_shift(token, 4)
    place = jnp.bitwise_and(token, 15)
    length = lent_ref[2:3, :]
    first = (block == lent_ref[0:1, :]) & (place < length)
    other = (block == lent_ref[1:2, :]) & (place + 16 < length)
    twice = first & other
    upper = jnp.where(first | other, jnp.where(twice, TWICE_HI, 0.0), DEAD)
    lower = jnp.where(twice, TWICE_LO, 0.0)
    out_ref[...] = jnp.where(iota((512, 128), 1) < SLOTS, upper, lower).astype(BF16)


HEADS = [(tt, h) for tt in range(2) for h in range(4)]


def pool(query, pick, keys, values, count):
    query = jnp.concatenate([query, jnp.concatenate([pick] * 8, axis=0)], axis=1)
    scores = dot_nt(query, keys)
    weights = []
    peaks = []
    for j in range(8):
        part = scores[j * count : (j + 1) * count]
        peak = jnp.max(part, axis=1, keepdims=True)
        weights.append(jnp.exp2((part - peak) * FACTOR).astype(BF16))
        peaks.append(peak)
    mixed = dot(jnp.concatenate(weights, axis=0), values)
    total = mixed[:, HD:]
    return (mixed[:, :HD] / total).astype(BF16), peaks, total


def columns(tt, peaks, total, count):
    lane = iota((count, 128), 1)
    top = jnp.zeros((count, 128), F32)
    amount = jnp.ones((count, 128), F32)
    for h in range(4):
        j = tt * 4 + h
        top = jnp.where(lane == h, peaks[j], top)
        amount = jnp.where(lane == h, total[j * count : (j + 1) * count], amount)
    lse = jnp.where(top > DEAD / 2, top * SCALE + jnp.log(amount), DEAD)
    return jnp.where(lane < 4, lse, 0.0)


def home_kernel(home_ref, first_ref, k_ref, v_ref, out_ref, lse_ref):
    token = iota((256, 128), 0)
    live = (jnp.right_shift(token, 4) == home_ref[0:1, :]) & (
        jnp.bitwise_and(token, 15) < home_ref[1:2, :]
    )
    mask = jnp.where(live, 0.0, DEAD).astype(BF16)
    pick = jnp.where(iota((ROWS, 128), 1) == iota((ROWS, 128), 0), 1.0, 0.0).astype(BF16)
    ones = jnp.ones((256, 128), BF16)
    for k in range(KVH):
        cut = slice(k * HD, (k + 1) * HD)
        keys = jnp.concatenate([k_ref[:, :, cut].reshape(256, HD), mask], axis=1)
        values = jnp.concatenate([v_ref[:, :, cut].reshape(256, HD), ones], axis=1)
        query = [first_ref[2 * k + tt, :, h * HD : (h + 1) * HD] for tt, h in HEADS]
        mixed, peaks, total = pool(jnp.concatenate(query, axis=0), pick, keys, values, ROWS)
        for tt in range(2):
            lse_ref[2 * k + tt] = columns(tt, peaks, total, ROWS)
        for j, (tt, h) in enumerate(HEADS):
            out_ref[2 * k + tt, head_rows(h), :] = mixed[j * ROWS : (j + 1) * ROWS]


def attend_kernel(x_ref, mask_ref, home_ref, home_lse_ref, k_ref, v_ref, out_ref):
    lane = iota((SLOTS, 128), 1)
    pick = jnp.where(
        jnp.bitwise_and(lane, SLOTS - 1) == iota((SLOTS, 128), 0), 1.0, 0.0
    ).astype(BF16)
    mask = mask_ref[...]
    ones = jnp.ones((512, 128), BF16)
    rest = jnp.zeros((ROWS, 128), F32)
    for k in range(KVH):
        cut = slice(k * HD, (k + 1) * HD)
        keys = jnp.concatenate([k_ref[:, :, cut].reshape(512, HD), mask], axis=1)
        values = jnp.concatenate([v_ref[:, :, cut].reshape(512, HD), ones], axis=1)
        query = [
            x_ref[d * N_TP + 2 * k + tt, :, h * HD : (h + 1) * HD]
            for tt, h in HEADS
            for d in range(2)
        ]
        mixed, peaks, total = pool(jnp.concatenate(query, axis=0), pick, keys, values, SLOTS)
        for tt in range(2):
            lse = columns(tt, peaks, total, SLOTS)
            home_lse = home_lse_ref[2 * k + tt]
            column = [lse[:HALF], home_lse, rest, lse[HALF:], home_lse, rest]
            lse = spread3(jnp.concatenate(column, axis=0)).T[:16]
            for d in range(2):
                to = d * N_TP + 2 * k + tt
                for h in range(4):
                    at = (tt * 4 + h) * SLOTS + d * HALF
                    out_ref[to, h * HALF : (h + 1) * HALF, :] = mixed[at : at + HALF]
                out_ref[to, 4 * HALF : PIECE - 16, :] = home_ref[
                    2 * k + tt, 2 * d * ROWS : 2 * (d + 1) * ROWS, :
                ]
                out_ref[to, PIECE - 16 :, :] = turn(lse, 64 * d).astype(BF16)


def merge_kernel(me_ref, target_ref, x_ref, out_ref, keep_ref, give_ref):
    core = jnp.bitwise_and(me_ref[0], 1)
    lane = iota((8, 128), 1)
    lses = []
    for t in range(2 * N_TP):
        parts = x_ref[t, PIECE - 16 :, :].astype(F32)
        lses.append(parts[0:4] + parts[4:8] + parts[8:12])
    lses = [jnp.concatenate([x, x], axis=0) for x in lses]

    def gather(sources, first):
        chunks = []
        for at in range(0, len(sources), 8):
            row = jnp.zeros((8, 128), F32)
            for j in range(8):
                moved = turn(lses[sources[at + j]], 16 * j - first)
                row = jnp.where(jnp.right_shift(lane, 4) == j, moved, row)
            chunks.append(row)
        return jnp.concatenate(chunks, axis=1)

    def join(mask, lse, values):
        score = jnp.where(mask, lse, DEAD)
        peak = jnp.max(score, axis=1, keepdims=True)
        weight = jnp.exp(score - peak)
        total = jnp.sum(weight, axis=1, keepdims=True)
        upper = weight.astype(BF16)
        lower = (weight - upper.astype(F32)).astype(BF16)
        both = dot(jnp.concatenate([upper, lower], axis=0), values)
        count = mask.shape[0]
        return (both[:count] + both[count:]) / total, peak + jnp.log(total)

    rows = iota((128, 512), 0).astype(F32)
    out_lane = iota((128, 128), 1)
    for g in range(2):
        lse = gather(list(range(2 * N_TP)), 16 * g)
        mask = rows == target_ref[g, 0:1, :]
        out_lse = jnp.zeros((128, 128), F32)
        block = slice(g * 8, (g + 1) * 8)
        for h in range(4):
            at = h * HALF + 16 * g
            values = x_ref[:, at : at + 16, :].reshape(512, HD)
            mixed, total = join(mask, lse[h : h + 1, :], values)
            out_lse = jnp.where(out_lane == h, total, out_lse)
            out_ref[block, head_rows(h), :] = mixed.astype(BF16).reshape(8, ROWS, HD)
        out_lse = fold(spread3(out_lse).reshape(8, ROWS, 128))
        out_ref[block, 4 * ROWS :, :] = out_lse.astype(BF16)
    mask = iota((ROWS, 256), 0) == jnp.bitwise_and(iota((ROWS, 256), 1), 15)
    home_lane = iota((ROWS, 128), 1)
    homes = []
    for d in range(2):
        lse = gather(list(range(d * N_TP, (d + 1) * N_TP)), HALF)
        lse = jnp.where(core == 0, lse[0:2], lse[2:4])
        out_lse = jnp.zeros((ROWS, 128), F32)
        parts = []
        for hh in range(2):
            at = 4 * HALF + hh * ROWS
            values = x_ref[d * N_TP : (d + 1) * N_TP, at : at + ROWS, :].reshape(256, HD)
            mixed, total = join(mask, lse[hh : hh + 1, :], values)
            parts.append(mixed)
            out_lse = jnp.where(home_lane == hh, total, out_lse)
        homes.append(jnp.concatenate(parts + [out_lse], axis=1))
    keep_ref[...] = jnp.where(core == 0, homes[0], homes[1])
    give_ref[...] = jnp.where(core == 0, homes[1], homes[0])


def final_kernel(me_ref, keep_ref, come_ref, x_ref, out_ref):
    core = jnp.bitwise_and(me_ref[0], 1)
    low = jnp.where(core == 0, keep_ref[...], come_ref[...])
    high = jnp.where(core == 0, come_ref[...], keep_ref[...])
    lane = iota((ROWS, 128), 1)
    lse = jnp.where(lane < 2, low[:, 2 * HD :], pltpu.roll(high[:, 2 * HD :], 2, 1))
    lses = [lse]
    for c in range(CHIPS):
        parts = unfold(x_ref[c, 4 * ROWS :, :].astype(F32))
        lses.append(parts + turn(parts, -4) + turn(parts, -8))
    peak = functools.reduce(jnp.maximum, lses)
    weights = [jnp.exp(lse - peak) for lse in lses]
    total = sum(weights)
    for h in range(4):
        home = (low if h < 2 else high)[:, (h % 2) * HD : (h % 2 + 1) * HD]
        mixed = weights[0][:, h : h + 1] * home
        for c in range(CHIPS):
            mixed = mixed + weights[c + 1][:, h : h + 1] * x_ref[c, head_rows(h), :].astype(F32)
        out_ref[:, h * HD : (h + 1) * HD] = (mixed / total[:, h : h + 1]).astype(BF16)


VMEM = pl.BlockSpec(memory_space=pltpu.VMEM)
SMEM = pl.BlockSpec(memory_space=pltpu.SMEM)
PARAMS = pltpu.CompilerParams(vmem_limit_bytes=24 * 1024 * 1024)


def exchange(x, axis, groups=None):
    return lax.all_to_all(
        x, axis, split_axis=0, concat_axis=0, axis_index_groups=groups, tiled=True
    )


def call(kernel, name, out_shape, args, smem=0):
    specs = [SMEM] * smem + [VMEM] * (len(args) - smem)
    return pl.pallas_call(
        kernel,
        out_shape=out_shape,
        in_specs=specs,
        out_specs=jax.tree.map(lambda _: VMEM, out_shape),
        compiler_params=PARAMS,
        name=name,
    )(*args)


def per_device(
    queries,
    home_keys,
    home_values,
    home_table,
    home_len,
    lent_keys,
    lent_values,
    lend_row,
    lend_table,
    lend_len,
):
    same_core = [[2 * z + core for z in range(CHIPS)] for core in range(2)]
    plane = [[(2 * z) * N_TP + j for j in range(2 * N_TP)] for z in range(CHIPS)]
    sibling = [(i, i ^ 1) for i in range(N_INST)]
    block = (CHIPS, 4 * ROWS + 8, HD)
    me = jnp.stack([lax.axis_index("inst"), lax.axis_index("tp")]).astype(jnp.int32)

    asked = jnp.pad(lend_row.reshape(N_INST, 2).T.astype(BF16), ((0, 0), (0, 128 - N_INST)))
    asked = jnp.broadcast_to(asked[None, :, None], (N_TP, 2, 8, 128)).reshape(N_TP, ROWS, 128)
    sent = jnp.broadcast_to(queries[None], (N_TP, ROWS, WIDTH))
    first = exchange(jnp.concatenate([sent, asked], axis=2), "tp")
    sent = call(spread_kernel, "spread", jax.ShapeDtypeStruct(block, BF16), (me, first), smem=1)
    mine = exchange(sent, "inst", same_core)

    meta = jnp.concatenate(
        [lend_table.reshape(CHIPS, 2, 2, 2), lend_len.reshape(CHIPS, 2, 2, 1)], axis=3
    )
    meta = meta.transpose(3, 1, 0, 2).reshape(3, SLOTS)
    mask = call(
        masks_kernel,
        "masks",
        jax.ShapeDtypeStruct((512, 128), BF16),
        (jnp.concatenate([meta, meta], axis=1),),
    )
    meta = jnp.concatenate([home_table.reshape(ROWS, 1), home_len], axis=1).T
    meta = jnp.pad(meta, ((0, 0), (0, 128 - ROWS)), constant_values=16)
    home, home_lse = call(
        home_kernel,
        "home",
        (
            jax.ShapeDtypeStruct((N_TP, 4 * ROWS, HD), BF16),
            jax.ShapeDtypeStruct((N_TP, ROWS, 128), F32),
        ),
        (meta, first, home_keys, home_values),
    )
    mine, mask, home, home_lse = lax.optimization_barrier((mine, mask, home, home_lse))

    picked, target = call(
        pick_kernel,
        "pick",
        (
            jax.ShapeDtypeStruct((2 * N_TP, HALF, WIDTH), BF16),
            jax.ShapeDtypeStruct((2, 8, 512), F32),
        ),
        (me, mine),
        smem=1,
    )
    arrived = exchange(picked, ("inst", "tp"), plane)
    partial = call(
        attend_kernel,
        "attend",
        jax.ShapeDtypeStruct((2 * N_TP, PIECE, HD), BF16),
        (arrived, mask, home, home_lse, lent_keys, lent_values),
    )
    returned = exchange(partial, ("inst", "tp"), plane)
    merged, keep, give = call(
        merge_kernel,
        "merge",
        (
            jax.ShapeDtypeStruct(block, BF16),
            jax.ShapeDtypeStruct((ROWS, 3 * HD), F32),
            jax.ShapeDtypeStruct((ROWS, 3 * HD), F32),
        ),
        (me, target, returned),
        smem=1,
    )
    come = lax.ppermute(give, "inst", sibling)
    back = exchange(merged, "inst", same_core)
    return call(
        final_kernel,
        "final",
        jax.ShapeDtypeStruct((ROWS, WIDTH), BF16),
        (me, keep, come, back),
        smem=1,
    )


def solution(mesh):
    in_specs = (
        P("inst", "tp"),
        P(("inst", "tp"), None, None),
        P(("inst", "tp"), None, None),
        P("inst", "tp", None),
        P("inst", "tp"),
        P(("inst", "tp"), None, None),
        P(("inst", "tp"), None, None),
        P("inst", None, "tp", None),
        P("inst", None, "tp", None, None),
        P("inst", None, "tp", None),
    )
    out_specs = P("inst", "tp")
    return jax.shard_map(
        per_device, mesh=mesh, in_specs=in_specs, out_specs=out_specs, check_vma=False
    )
```

```python
import functools
import math

import jax
import jax.numpy as jnp
import ml_dtypes
import numpy as np
from jax import lax
from jax.experimental import pallas as pl
from jax.experimental.pallas import tpu as pltpu
from jax.sharding import PartitionSpec as P

QH = 64
KVH = 8
HD = 128
N_INST = 32
N_TP = 16
ROWS = 16
SLOTS = 64
WIDTH = 512
CHIPS = N_INST // 2
HALF = SLOTS // 2
PIECE = 4 * HALF + 2 * ROWS + 16
DEAD = -1e30
SCALE = HD ** (-0.5)
F32 = jnp.float32
BF16 = jnp.bfloat16
FACTOR = SCALE * math.log2(math.e)
TWICE_HI = float(np.float32(1 / FACTOR).astype(ml_dtypes.bfloat16))
TWICE_LO = 1 / FACTOR - TWICE_HI


def iota(shape, axis):
    return lax.broadcasted_iota(jnp.int32, shape, axis)


def dot(a, b):
    return jnp.dot(a, b, preferred_element_type=F32)


def dot_nt(a, b):
    return lax.dot_general(a, b, (((1,), (1,)), ((), ())), preferred_element_type=F32)


def split3(x):
    hi = x.astype(BF16).astype(F32)
    rest = x - hi
    mid = rest.astype(BF16).astype(F32)
    return hi, mid, rest - mid


def thirds(x, lane):
    hi, mid, low = split3(x)
    return jnp.where(lane < 4, hi, jnp.where(lane < 8, mid, jnp.where(lane < 12, low, 0.0)))


def head_rows(h):
    return slice(h * ROWS, (h + 1) * ROWS)


def spread_kernel(me_ref, first_ref, out_ref, block_s, sems):
    row = iota((8, 128), 0)
    quarters = []
    for half in range(2):
        for s in range(2):
            asked = jnp.zeros((8, 128), F32)
            for t in range(8):
                part = first_ref[8 * half + t, :, WIDTH:].astype(F32)
                asked = jnp.where(row == t, part[8 * s : 8 * (s + 1)], asked)
            quarters.append(asked)
    asked = quarters[0]
    for j in range(1, 4):
        asked = asked + pltpu.roll(quarters[j], j * N_INST, 1)
    queries = jnp.zeros((ROWS, WIDTH), F32)
    for t in range(N_TP):
        own = jnp.concatenate([me_ref[1]] * 2, axis=0)[:, :1] == t
        queries = jnp.where(own, first_ref[t, :, :WIDTH].astype(F32), queries)
    queries = queries.astype(BF16)
    for h in range(4):
        block_s[head_rows(h), :] = queries[:, h * HD : (h + 1) * HD]
    block_s[4 * ROWS :, :] = asked.astype(BF16)
    copies = [pltpu.make_async_copy(block_s, out_ref.at[z], sems.at[z]) for z in range(CHIPS)]
    for copy in copies:
        copy.start()
    for copy in copies:
        copy.wait()


def places(me, mine_ref, g):
    k = iota((256, 128), 0)
    n = iota((256, 128), 1)
    local = jnp.bitwise_and(jnp.right_shift(k, 1), 7)
    source = local * 8 + jnp.bitwise_and(jnp.right_shift(k, 4), 7)
    order = jnp.where(n == source, 1.0, 0.0).astype(BF16)
    asked = mine_ref[g * 8 : (g + 1) * 8, 4 * ROWS :, :].astype(F32).reshape(64, 128)
    asked = dot(order[:, :64], asked.astype(BF16))
    column = 2 * N_INST * jnp.right_shift(k, 7) + N_INST * jnp.bitwise_and(k, 1)
    column = column + 2 * jnp.right_shift(me, 1)
    ones = jnp.ones((128, 128), BF16)
    base = local.astype(F32) * 16.0
    return [
        dot(jnp.where(n == column + d, asked, 0.0).astype(BF16), ones) + base
        for d in range(2)
    ]


def pick_kernel(me_ref, mine_ref, out_ref, target_ref):
    lane = iota((256, 128), 1).astype(F32)
    for g in range(2):
        block = jnp.concatenate(
            [
                mine_ref[g * 8 : (g + 1) * 8, head_rows(h), :].reshape(128, HD)
                for h in range(4)
            ],
            axis=1,
        )
        for d, target in enumerate(places(me_ref[0, :1], mine_ref, g)):
            onehot = jnp.where(lane == target, 1.0, 0.0).astype(BF16)
            picked = dot(onehot, block).astype(BF16)
            out_ref[d * N_TP : (d + 1) * N_TP, g * 16 : (g + 1) * 16, :] = picked.reshape(
                N_TP, 16, WIDTH
            )
            target_ref[g, :, d * 256 : (d + 1) * 256] = target.T[:8]


def masks_kernel(lent_ref, out_ref):
    token = iota((512, 128), 0)
    block = jnp.right_shift(token, 4)
    place = jnp.bitwise_and(token, 15)
    length = lent_ref[2:3, :]
    first = (block == lent_ref[0:1, :]) & (place < length)
    other = (block == lent_ref[1:2, :]) & (place + 16 < length)
    twice = first & other
    upper = jnp.where(first | other, jnp.where(twice, TWICE_HI, 0.0), DEAD)
    lower = jnp.where(twice, TWICE_LO, 0.0)
    out_ref[...] = jnp.where(iota((512, 128), 1) < SLOTS, upper, lower).astype(BF16)


HEADS = [(tt, h) for tt in range(2) for h in range(4)]


def pool(query, pick, keys, values, count):
    query = jnp.concatenate([query, jnp.concatenate([pick] * 8, axis=0)], axis=1)
    scores = dot_nt(query, keys)
    weights = []
    peaks = []
    for j in range(8):
        part = scores[j * count : (j + 1) * count]
        peak = jnp.max(part, axis=1, keepdims=True)
        weights.append(jnp.exp2((part - peak) * FACTOR).astype(BF16))
        peaks.append(peak)
    mixed = dot(jnp.concatenate(weights, axis=0), values)
    total = mixed[:, HD:]
    return (mixed[:, :HD] / total).astype(BF16), peaks, total


def columns(tt, peaks, total, count):
    head = jnp.bitwise_and(iota((count, 128), 1), 3)
    top = jnp.zeros((count, 128), F32)
    amount = jnp.ones((count, 128), F32)
    for h in range(4):
        j = tt * 4 + h
        top = jnp.where(head == h, peaks[j], top)
        amount = jnp.where(head == h, total[j * count : (j + 1) * count], amount)
    return jnp.where(top > DEAD / 2, top * SCALE + jnp.log(amount), DEAD)


def home_kernel(home_ref, first_ref, k_ref, v_ref, out_ref, lse_ref):
    token = iota((256, 128), 0)
    live = (jnp.right_shift(token, 4) == home_ref[0:1, :]) & (
        jnp.bitwise_and(token, 15) < home_ref[1:2, :]
    )
    mask = jnp.where(live, 0.0, DEAD).astype(BF16)
    pick = jnp.where(iota((ROWS, 128), 1) == iota((ROWS, 128), 0), 1.0, 0.0).astype(BF16)
    ones = jnp.ones((256, 128), BF16)
    for k in range(KVH):
        cut = slice(k * HD, (k + 1) * HD)
        keys = jnp.concatenate([k_ref[:, :, cut].reshape(256, HD), mask], axis=1)
        values = jnp.concatenate([v_ref[:, :, cut].reshape(256, HD), ones], axis=1)
        query = [first_ref[2 * k + tt, :, h * HD : (h + 1) * HD] for tt, h in HEADS]
        mixed, peaks, total = pool(jnp.concatenate(query, axis=0), pick, keys, values, ROWS)
        for tt in range(2):
            lse_ref[2 * k + tt] = columns(tt, peaks, total, ROWS)
        for j, (tt, h) in enumerate(HEADS):
            out_ref[2 * k + tt, head_rows(h), :] = mixed[j * ROWS : (j + 1) * ROWS]


def attend_kernel(x_ref, mask_ref, home_ref, home_lse_ref, k_ref, v_ref, out_ref):
    lane = iota((SLOTS, 128), 1)
    pick = jnp.where(
        jnp.bitwise_and(lane, SLOTS - 1) == iota((SLOTS, 128), 0), 1.0, 0.0
    ).astype(BF16)
    mask = mask_ref[...]
    ones = jnp.ones((512, 128), BF16)
    rest = jnp.zeros((ROWS, 128), F32)
    for k in range(KVH):
        cut = slice(k * HD, (k + 1) * HD)
        keys = jnp.concatenate([k_ref[:, :, cut].reshape(512, HD), mask], axis=1)
        values = jnp.concatenate([v_ref[:, :, cut].reshape(512, HD), ones], axis=1)
        query = [
            x_ref[d * N_TP + 2 * k + tt, :, h * HD : (h + 1) * HD]
            for tt, h in HEADS
            for d in range(2)
        ]
        mixed, peaks, total = pool(jnp.concatenate(query, axis=0), pick, keys, values, SLOTS)
        for tt in range(2):
            lse = columns(tt, peaks, total, SLOTS)
            home_lse = home_lse_ref[2 * k + tt]
            column = [lse[:HALF], home_lse, rest, lse[HALF:], home_lse, rest]
            lse = thirds(jnp.concatenate(column, axis=0), iota((128, 128), 1)).T[:16].astype(BF16)
            for d in range(2):
                to = d * N_TP + 2 * k + tt
                for h in range(4):
                    at = (tt * 4 + h) * SLOTS + d * HALF
                    out_ref[to, h * HALF : (h + 1) * HALF, :] = mixed[at : at + HALF]
                out_ref[to, 4 * HALF : PIECE - 16, :] = home_ref[
                    2 * k + tt, 2 * d * ROWS : 2 * (d + 1) * ROWS, :
                ]
                out_ref[to, PIECE - 16 :, :] = lse


def merge_kernel(me_ref, target_ref, x_ref, out_ref, keep_ref, give_ref):
    core = jnp.bitwise_and(me_ref[0, :1], 1)
    rows = [
        jnp.concatenate(
            [x_ref[8 * chunk + j, PIECE - 16 :, :] for j in range(8)], axis=1
        )
        for chunk in range(4)
    ]
    k = iota((1024, 3 * 128), 0)
    n = iota((1024, 3 * 128), 1)
    place = jnp.bitwise_and(n, 127)
    source = 128 * jnp.right_shift(place, 4) + 64 * jnp.concatenate([core] * 3, axis=1)
    source = source + 16 * jnp.right_shift(n, 7) + jnp.bitwise_and(place, 15)
    moved = dot(jnp.concatenate(rows, axis=0), jnp.where(k == source, 1.0, 0.0).astype(BF16))
    lses = []
    for chunk in range(4):
        part = moved[16 * chunk : 16 * (chunk + 1)]
        lses.append(part[0:4] + part[4:8] + part[8:12])

    def gather(group, chunks):
        cut = slice(group * 128, (group + 1) * 128)
        return jnp.concatenate([lses[chunk][:, cut] for chunk in chunks], axis=1)

    ones = jnp.ones((512, HD), BF16)

    def join(mask, lse, values):
        score = jnp.where(mask, lse, DEAD)
        peak = jnp.max(score, axis=1, keepdims=True)
        weight = jnp.exp(score - peak)
        upper = weight.astype(BF16)
        lower = (weight - upper.astype(F32)).astype(BF16)
        values = jnp.concatenate([values, ones[: values.shape[0]]], axis=1)
        both = dot(jnp.concatenate([upper, lower], axis=0), values)
        count = mask.shape[0]
        both = both[:count] + both[count:]
        return both[:, :HD] / both[:, HD:], peak + jnp.log(both[:, HD:])

    rows = iota((128, 512), 0).astype(F32)
    row = jnp.bitwise_and(iota((128, 128), 0), 8)
    lane = iota((128, 128), 1) - 8 * row
    head = jnp.bitwise_and(lane, 3)
    for g in range(2):
        lse = gather(g, range(4))
        mask = rows == target_ref[g, 0:1, :]
        out_lse = jnp.zeros((128, 128), F32)
        block = slice(g * 8, (g + 1) * 8)
        for h in range(4):
            at = h * HALF + 16 * g
            values = x_ref[:, at : at + 16, :].reshape(512, HD)
            mixed, total = join(mask, lse[h : h + 1, :], values)
            out_lse = jnp.where(head == h, total, out_lse)
            out_ref[block, head_rows(h), :] = mixed.astype(BF16).reshape(8, ROWS, HD)
        out_lse = jnp.where(lane >= 0, thirds(out_lse, lane), 0.0).reshape(8, ROWS, 128)
        out_ref[block, 4 * ROWS :, :] = (out_lse[:, :8] + out_lse[:, 8:]).astype(BF16)
    mask = iota((ROWS, 256), 0) == jnp.bitwise_and(iota((ROWS, 256), 1), 15)
    homes = []
    for d in range(2):
        lse = gather(2, range(2 * d, 2 * d + 2))
        lse = jnp.where(core[:, :1] == 0, lse[0:2], lse[2:4])
        parts = []
        for hh in range(2):
            at = 4 * HALF + hh * ROWS
            values = x_ref[d * N_TP : (d + 1) * N_TP, at : at + ROWS, :].reshape(256, HD)
            parts.extend(join(mask, lse[hh : hh + 1, :], values))
        homes.append(jnp.concatenate(parts, axis=1))
    keep_ref[...] = jnp.where(core[:, :1] == 0, homes[0], homes[1])
    give_ref[...] = jnp.where(core[:, :1] == 0, homes[1], homes[0])


def final_kernel(me_ref, keep_ref, come_ref, x_ref, out_ref):
    core = jnp.bitwise_and(me_ref[0, :1], 1)
    low = jnp.where(core[:, :1] == 0, keep_ref[...], come_ref[...])
    high = jnp.where(core[:, :1] == 0, come_ref[...], keep_ref[...])
    blocks = [x_ref[c].astype(F32) for c in range(CHIPS)]
    n = iota((128, 1024), 1)
    lane = iota((128, 1024), 0) - 64 * jnp.right_shift(n, 9)
    head = jnp.bitwise_and(jnp.right_shift(n, 7), 3)
    part = (lane >= 0) & (lane < 12) & (jnp.bitwise_and(lane, 3) == head)
    lses = jnp.concatenate([block[4 * ROWS :] for block in blocks], axis=0).astype(BF16)
    lses = dot(lses, jnp.where(part, 1.0, 0.0).astype(BF16))
    for h in range(4):
        home = (low if h < 2 else high)[:, (h % 2) * 2 * HD : (h % 2 + 1) * 2 * HD]
        halves = []
        for half in range(2):
            at = (half * 4 + h) * 128
            rows = slice(half * 8, (half + 1) * 8)
            parts = [lses[c * 8 : (c + 1) * 8, at : at + 128] for c in range(CHIPS)]
            peak = functools.reduce(jnp.maximum, parts, home[rows, HD:])
            total = jnp.exp(home[rows, HD:] - peak)
            mixed = total * home[rows, :HD]
            for c in range(CHIPS):
                weight = jnp.exp(parts[c] - peak)
                total = total + weight
                at = h * ROWS + half * 8
                mixed = mixed + weight * blocks[c][at : at + 8]
            halves.append(mixed / total)
        out_ref[:, h * HD : (h + 1) * HD] = jnp.concatenate(halves, axis=0).astype(BF16)


VMEM = pl.BlockSpec(memory_space=pltpu.VMEM)
PARAMS = pltpu.CompilerParams(vmem_limit_bytes=24 * 1024 * 1024)


def exchange(x, axis, groups=None):
    return lax.all_to_all(
        x, axis, split_axis=0, concat_axis=0, axis_index_groups=groups, tiled=True
    )


def call(kernel, name, out_shape, args):
    return pl.pallas_call(
        kernel,
        out_shape=out_shape,
        in_specs=[VMEM] * len(args),
        out_specs=jax.tree.map(lambda _: VMEM, out_shape),
        compiler_params=PARAMS,
        name=name,
    )(*args)


def per_device(
    queries,
    home_keys,
    home_values,
    home_table,
    home_len,
    lent_keys,
    lent_values,
    lend_row,
    lend_table,
    lend_len,
):
    same_core = [[2 * z + core for z in range(CHIPS)] for core in range(2)]
    plane = [[(2 * z) * N_TP + j for j in range(2 * N_TP)] for z in range(CHIPS)]
    sibling = [(i, i ^ 1) for i in range(N_INST)]
    block = (CHIPS, 4 * ROWS + 8, HD)
    me = jnp.stack([lax.axis_index("inst"), lax.axis_index("tp")]).astype(jnp.int32)
    me = jnp.broadcast_to(me[:, None, None], (2, 8, 128))

    asked = jnp.pad(lend_row.reshape(N_INST, 2).T.astype(BF16), ((0, 0), (0, 128 - N_INST)))
    asked = jnp.broadcast_to(asked[:, None], (2, 8, 128)).reshape(ROWS, 128)
    sent, me = lax.optimization_barrier((jnp.concatenate([queries, asked], axis=1), me))
    sent = jnp.broadcast_to(sent[None], (N_TP, ROWS, WIDTH + 128))
    first = exchange(sent, "tp")
    sent = pl.pallas_call(
        spread_kernel,
        out_shape=jax.ShapeDtypeStruct(block, BF16),
        in_specs=[VMEM, VMEM],
        out_specs=pl.BlockSpec(memory_space=pl.ANY),
        scratch_shapes=[pltpu.VMEM(block[1:], BF16), pltpu.SemaphoreType.DMA((CHIPS,))],
        compiler_params=PARAMS,
        name="spread",
    )(me, first)
    mine = exchange(sent, "inst", same_core)

    meta = jnp.concatenate(
        [lend_table.reshape(CHIPS, 2, 2, 2), lend_len.reshape(CHIPS, 2, 2, 1)], axis=3
    )
    meta = meta.transpose(3, 1, 0, 2).reshape(3, SLOTS)
    mask = call(
        masks_kernel,
        "masks",
        jax.ShapeDtypeStruct((512, 128), BF16),
        (jnp.concatenate([meta, meta], axis=1),),
    )
    meta = jnp.concatenate([home_table.reshape(ROWS, 1), home_len], axis=1).T
    meta = jnp.pad(meta, ((0, 0), (0, 128 - ROWS)), constant_values=16)
    home, home_lse = call(
        home_kernel,
        "home",
        (
            jax.ShapeDtypeStruct((N_TP, 4 * ROWS, HD), BF16),
            jax.ShapeDtypeStruct((N_TP, ROWS, 128), F32),
        ),
        (meta, first, home_keys, home_values),
    )
    mine, mask, home, home_lse = lax.optimization_barrier((mine, mask, home, home_lse))

    picked, target = call(
        pick_kernel,
        "pick",
        (
            jax.ShapeDtypeStruct((2 * N_TP, HALF, WIDTH), BF16),
            jax.ShapeDtypeStruct((2, 8, 512), F32),
        ),
        (me, mine),
    )
    arrived = exchange(picked, ("inst", "tp"), plane)
    partial = call(
        attend_kernel,
        "attend",
        jax.ShapeDtypeStruct((2 * N_TP, PIECE, HD), BF16),
        (arrived, mask, home, home_lse, lent_keys, lent_values),
    )
    returned = exchange(partial, ("inst", "tp"), plane)
    merged, keep, give = call(
        merge_kernel,
        "merge",
        (
            jax.ShapeDtypeStruct(block, BF16),
            jax.ShapeDtypeStruct((ROWS, 4 * HD), F32),
            jax.ShapeDtypeStruct((ROWS, 4 * HD), F32),
        ),
        (me, target, returned),
    )
    come = lax.ppermute(give, "inst", sibling)
    back = exchange(merged, "inst", same_core)
    return call(
        final_kernel,
        "final",
        jax.ShapeDtypeStruct((ROWS, WIDTH), BF16),
        (me, keep, come, back),
    )


def solution(mesh):
    in_specs = (
        P("inst", "tp"),
        P(("inst", "tp"), None, None),
        P(("inst", "tp"), None, None),
        P("inst", "tp", None),
        P("inst", "tp"),
        P(("inst", "tp"), None, None),
        P(("inst", "tp"), None, None),
        P("inst", None, "tp", None),
        P("inst", None, "tp", None, None),
        P("inst", None, "tp", None),
    )
    out_specs = P("inst", "tp")
    return jax.shard_map(
        per_device, mesh=mesh, in_specs=in_specs, out_specs=out_specs, check_vma=False
    )
```

```python
import functools
import math

import jax
import jax.numpy as jnp
import ml_dtypes
import numpy as np
from jax import lax
from jax.experimental import pallas as pl
from jax.experimental.pallas import tpu as pltpu
from jax.sharding import PartitionSpec as P

QH = 64
KVH = 8
HD = 128
N_INST = 32
N_TP = 16
ROWS = 16
SLOTS = 64
WIDTH = 512
CHIPS = N_INST // 2
HALF = SLOTS // 2
PIECE = 4 * HALF + 2 * ROWS + 8
DEAD = -1e30
SCALE = HD ** (-0.5)
F32 = jnp.float32
BF16 = jnp.bfloat16
FACTOR = SCALE * math.log2(math.e)
TWICE_HI = float(np.float32(1 / FACTOR).astype(ml_dtypes.bfloat16))
TWICE_LO = 1 / FACTOR - TWICE_HI


def iota(shape, axis):
    return lax.broadcasted_iota(jnp.int32, shape, axis)


def dot(a, b):
    return jnp.dot(a, b, preferred_element_type=F32)


def dot_nt(a, b):
    return lax.dot_general(a, b, (((1,), (1,)), ((), ())), preferred_element_type=F32)


def split3(x):
    hi = x.astype(BF16).astype(F32)
    rest = x - hi
    mid = rest.astype(BF16).astype(F32)
    return hi, mid, rest - mid


def thirds(x, lane):
    hi, mid, low = split3(x)
    return jnp.where(lane < 4, hi, jnp.where(lane < 8, mid, jnp.where(lane < 12, low, 0.0)))


def head_rows(h):
    return slice(h * ROWS, (h + 1) * ROWS)


def spread_kernel(me_ref, first_ref, out_ref, block_s, sems):
    row = iota((8, 128), 0)
    quarters = []
    for half in range(2):
        for s in range(2):
            asked = jnp.zeros((8, 128), F32)
            for t in range(8):
                part = first_ref[8 * half + t, :, WIDTH:].astype(F32)
                asked = jnp.where(row == t, part[8 * s : 8 * (s + 1)], asked)
            quarters.append(asked)
    asked = quarters[0]
    for j in range(1, 4):
        asked = asked + pltpu.roll(quarters[j], j * N_INST, 1)
    queries = jnp.zeros((ROWS, WIDTH), F32)
    for t in range(N_TP):
        own = jnp.concatenate([me_ref[1]] * 2, axis=0)[:, :1] == t
        queries = jnp.where(own, first_ref[t, :, :WIDTH].astype(F32), queries)
    queries = queries.astype(BF16)
    for h in range(4):
        block_s[head_rows(h), :] = queries[:, h * HD : (h + 1) * HD]
    block_s[4 * ROWS :, :] = asked.astype(BF16)
    copies = [pltpu.make_async_copy(block_s, out_ref.at[z], sems.at[z]) for z in range(CHIPS)]
    for copy in copies:
        copy.start()
    for copy in copies:
        copy.wait()


def places(me, mine_ref, g):
    k = iota((256, 128), 0)
    n = iota((256, 128), 1)
    local = jnp.bitwise_and(jnp.right_shift(k, 1), 7)
    source = local * 8 + jnp.bitwise_and(jnp.right_shift(k, 4), 7)
    order = jnp.where(n == source, 1.0, 0.0).astype(BF16)
    asked = mine_ref[g * 8 : (g + 1) * 8, 4 * ROWS :, :].astype(F32).reshape(64, 128)
    asked = dot(order[:, :64], asked.astype(BF16))
    column = 2 * N_INST * jnp.right_shift(k, 7) + N_INST * jnp.bitwise_and(k, 1)
    column = column + 2 * jnp.right_shift(me, 1)
    ones = jnp.ones((128, 128), BF16)
    base = local.astype(F32) * 16.0
    return [
        dot(jnp.where(n == column + d, asked, 0.0).astype(BF16), ones) + base
        for d in range(2)
    ]


def pick_kernel(me_ref, mine_ref, out_ref, target_ref):
    lane = iota((256, 128), 1).astype(F32)
    for g in range(2):
        block = jnp.concatenate(
            [
                mine_ref[g * 8 : (g + 1) * 8, head_rows(h), :].reshape(128, HD)
                for h in range(4)
            ],
            axis=1,
        )
        for d, target in enumerate(places(me_ref[0, :1], mine_ref, g)):
            onehot = jnp.where(lane == target, 1.0, 0.0).astype(BF16)
            picked = dot(onehot, block).astype(BF16)
            out_ref[d * N_TP : (d + 1) * N_TP, g * 16 : (g + 1) * 16, :] = picked.reshape(
                N_TP, 16, WIDTH
            )
            target_ref[g, :, d * 256 : (d + 1) * 256] = target.T[:8]


def masks_kernel(lent_ref, out_ref):
    token = iota((512, 128), 0)
    block = jnp.right_shift(token, 4)
    place = jnp.bitwise_and(token, 15)
    length = lent_ref[2:3, :]
    first = (block == lent_ref[0:1, :]) & (place < length)
    other = (block == lent_ref[1:2, :]) & (place + 16 < length)
    twice = first & other
    upper = jnp.where(first | other, jnp.where(twice, TWICE_HI, 0.0), DEAD)
    lower = jnp.where(twice, TWICE_LO, 0.0)
    out_ref[...] = jnp.where(iota((512, 128), 1) < SLOTS, upper, lower).astype(BF16)


HEADS = [(tt, h) for tt in range(2) for h in range(4)]


def pool(query, pick, keys, values, count):
    query = jnp.concatenate([query, jnp.concatenate([pick] * 8, axis=0)], axis=1)
    scores = dot_nt(query, keys)
    weights = []
    peaks = []
    for j in range(8):
        part = scores[j * count : (j + 1) * count]
        peak = jnp.max(part, axis=1, keepdims=True)
        weights.append(jnp.exp2((part - peak) * FACTOR).astype(BF16))
        peaks.append(peak)
    mixed = dot(jnp.concatenate(weights, axis=0), values)
    total = mixed[:, HD:]
    return (mixed[:, :HD] / total).astype(BF16), peaks, total


def columns(tt, peaks, total, count):
    head = jnp.bitwise_and(iota((count, 128), 1), 3)
    top = jnp.zeros((count, 128), F32)
    amount = jnp.ones((count, 128), F32)
    for h in range(4):
        j = tt * 4 + h
        top = jnp.where(head == h, peaks[j], top)
        amount = jnp.where(head == h, total[j * count : (j + 1) * count], amount)
    return jnp.where(top > DEAD / 2, top * SCALE + jnp.log(amount), DEAD)


def home_kernel(home_ref, first_ref, k_ref, v_ref, out_ref, lse_ref):
    token = iota((256, 128), 0)
    live = (jnp.right_shift(token, 4) == home_ref[0:1, :]) & (
        jnp.bitwise_and(token, 15) < home_ref[1:2, :]
    )
    mask = jnp.where(live, 0.0, DEAD).astype(BF16)
    pick = jnp.where(iota((ROWS, 128), 1) == iota((ROWS, 128), 0), 1.0, 0.0).astype(BF16)
    ones = jnp.ones((256, 128), BF16)
    for k in range(KVH):
        cut = slice(k * HD, (k + 1) * HD)
        keys = jnp.concatenate([k_ref[:, :, cut].reshape(256, HD), mask], axis=1)
        values = jnp.concatenate([v_ref[:, :, cut].reshape(256, HD), ones], axis=1)
        query = [first_ref[2 * k + tt, :, h * HD : (h + 1) * HD] for tt, h in HEADS]
        mixed, peaks, total = pool(jnp.concatenate(query, axis=0), pick, keys, values, ROWS)
        for tt in range(2):
            lse_ref[2 * k + tt] = columns(tt, peaks, total, ROWS)
        for j, (tt, h) in enumerate(HEADS):
            out_ref[2 * k + tt, head_rows(h), :] = mixed[j * ROWS : (j + 1) * ROWS]


def attend_kernel(x_ref, mask_ref, home_ref, home_lse_ref, k_ref, v_ref, out_ref):
    lane = iota((SLOTS, 128), 1)
    pick = jnp.where(
        jnp.bitwise_and(lane, SLOTS - 1) == iota((SLOTS, 128), 0), 1.0, 0.0
    ).astype(BF16)
    mask = mask_ref[...]
    ones = jnp.ones((512, 128), BF16)
    rest = jnp.zeros((ROWS, 128), F32)
    for k in range(KVH):
        cut = slice(k * HD, (k + 1) * HD)
        keys = jnp.concatenate([k_ref[:, :, cut].reshape(512, HD), mask], axis=1)
        values = jnp.concatenate([v_ref[:, :, cut].reshape(512, HD), ones], axis=1)
        query = [
            x_ref[d * N_TP + 2 * k + tt, :, h * HD : (h + 1) * HD]
            for tt, h in HEADS
            for d in range(2)
        ]
        mixed, peaks, total = pool(jnp.concatenate(query, axis=0), pick, keys, values, SLOTS)
        for tt in range(2):
            lse = columns(tt, peaks, total, SLOTS)
            home_lse = home_lse_ref[2 * k + tt]
            column = [lse[:HALF], home_lse, rest, lse[HALF:], home_lse, rest]
            lse = thirds(jnp.concatenate(column, axis=0), iota((128, 128), 1)).T
            other = pltpu.roll(lse[:16], 64, 1)
            near = iota((8, 128), 1) < 64
            for d in range(2):
                to = d * N_TP + 2 * k + tt
                for h in range(4):
                    at = (tt * 4 + h) * SLOTS + d * HALF
                    out_ref[to, h * HALF : (h + 1) * HALF, :] = mixed[at : at + HALF]
                out_ref[to, 4 * HALF : PIECE - 8, :] = home_ref[
                    2 * k + tt, 2 * d * ROWS : 2 * (d + 1) * ROWS, :
                ]
                pair = (other[:8], lse[8:16]) if d else (lse[:8], other[8:])
                out_ref[to, PIECE - 8 :, :] = jnp.where(near, *pair).astype(BF16)


def settled(x_ref, groups):
    wide = 2 * len(groups) * 128
    k = iota((128, wide), 0)
    n = iota((128, wide), 1)
    source = 64 * jnp.bitwise_and(jnp.right_shift(n, 7), 1) + jnp.bitwise_and(n, 15)
    for j, group in enumerate(groups):
        source = source + jnp.where(jnp.right_shift(n, 8) == j, 16 * group, 0)
    rows = x_ref[:, PIECE - 8 :, :].astype(F32).reshape(2 * N_TP * 8, 128).astype(BF16)
    moved = dot(rows, jnp.where(k == source, 1.0, 0.0).astype(BF16))
    place = jnp.right_shift(iota((8, 128), 1), 4)

    def settle(chunk, part):
        row = jnp.zeros((8, 128), F32)
        for j in range(8):
            at = (8 * chunk + j) * 8
            row = jnp.where(place == j, moved[at : at + 8, part * 128 : (part + 1) * 128], row)
        return row

    out = []
    for j in range(len(groups)):
        chunks = []
        for chunk in range(4):
            upper = settle(chunk, 2 * j)
            chunks.append(upper[0:4] + upper[4:8] + settle(chunk, 2 * j + 1)[0:4])
        out.append(chunks)
    return out


def join(mask, lse, values):
    score = jnp.where(mask, lse, DEAD)
    peak = jnp.max(score, axis=1, keepdims=True)
    weight = jnp.exp(score - peak)
    upper = weight.astype(BF16)
    lower = (weight - upper.astype(F32)).astype(BF16)
    values = jnp.concatenate([values, jnp.ones(values.shape, BF16)], axis=1)
    both = dot(jnp.concatenate([upper, lower], axis=0), values)
    count = mask.shape[0]
    both = both[:count] + both[count:]
    return both[:, :HD] / both[:, HD:], peak + jnp.log(both[:, HD:])


def merge_kernel(target_ref, x_ref, out_ref):
    lses = settled(x_ref, (0, 1))
    rows = iota((128, 512), 0).astype(F32)
    row = jnp.bitwise_and(iota((128, 128), 0), 8)
    lane = iota((128, 128), 1) - 8 * row
    head = jnp.bitwise_and(lane, 3)
    for g in range(2):
        lse = jnp.concatenate(lses[g], axis=1)
        mask = rows == target_ref[g, 0:1, :]
        out_lse = jnp.zeros((128, 128), F32)
        block = slice(g * 8, (g + 1) * 8)
        for h in range(4):
            at = h * HALF + 16 * g
            values = x_ref[:, at : at + 16, :].reshape(512, HD)
            mixed, total = join(mask, lse[h : h + 1, :], values)
            out_lse = jnp.where(head == h, total, out_lse)
            out_ref[block, head_rows(h), :] = mixed.astype(BF16).reshape(8, ROWS, HD)
        out_lse = jnp.where(lane >= 0, thirds(out_lse, lane), 0.0).reshape(8, ROWS, 128)
        out_ref[block, 4 * ROWS :, :] = (out_lse[:, :8] + out_lse[:, 8:]).astype(BF16)


def home_merge_kernel(me_ref, x_ref, keep_ref, give_ref):
    core = jnp.bitwise_and(me_ref[0, :1], 1)
    lses = settled(x_ref, (2,))[0]
    mask = iota((ROWS, 256), 0) == jnp.bitwise_and(iota((ROWS, 256), 1), 15)
    homes = []
    for d in range(2):
        lse = jnp.concatenate(lses[2 * d : 2 * d + 2], axis=1)
        lse = jnp.where(core[:, :1] == 0, lse[0:2], lse[2:4])
        parts = []
        for hh in range(2):
            at = 4 * HALF + hh * ROWS
            values = x_ref[d * N_TP : (d + 1) * N_TP, at : at + ROWS, :].reshape(256, HD)
            parts.extend(join(mask, lse[hh : hh + 1, :], values))
        homes.append(jnp.concatenate(parts, axis=1))
    keep_ref[...] = jnp.where(core[:, :1] == 0, homes[0], homes[1])
    give_ref[...] = jnp.where(core[:, :1] == 0, homes[1], homes[0])


def final_kernel(me_ref, keep_ref, come_ref, x_ref, out_ref):
    core = jnp.bitwise_and(me_ref[0, :1], 1)
    low = jnp.where(core[:, :1] == 0, keep_ref[...], come_ref[...])
    high = jnp.where(core[:, :1] == 0, come_ref[...], keep_ref[...])
    blocks = [x_ref[c].astype(F32) for c in range(CHIPS)]
    n = iota((128, 1024), 1)
    lane = iota((128, 1024), 0) - 64 * jnp.right_shift(n, 9)
    head = jnp.bitwise_and(jnp.right_shift(n, 7), 3)
    part = (lane >= 0) & (lane < 12) & (jnp.bitwise_and(lane, 3) == head)
    lses = jnp.concatenate([block[4 * ROWS :] for block in blocks], axis=0).astype(BF16)
    lses = dot(lses, jnp.where(part, 1.0, 0.0).astype(BF16))
    for h in range(4):
        home = (low if h < 2 else high)[:, (h % 2) * 2 * HD : (h % 2 + 1) * 2 * HD]
        halves = []
        for half in range(2):
            at = (half * 4 + h) * 128
            rows = slice(half * 8, (half + 1) * 8)
            parts = [lses[c * 8 : (c + 1) * 8, at : at + 128] for c in range(CHIPS)]
            peak = functools.reduce(jnp.maximum, parts, home[rows, HD:])
            total = jnp.exp(home[rows, HD:] - peak)
            mixed = total * home[rows, :HD]
            for c in range(CHIPS):
                weight = jnp.exp(parts[c] - peak)
                total = total + weight
                at = h * ROWS + half * 8
                mixed = mixed + weight * blocks[c][at : at + 8]
            halves.append(mixed / total)
        out_ref[:, h * HD : (h + 1) * HD] = jnp.concatenate(halves, axis=0).astype(BF16)


VMEM = pl.BlockSpec(memory_space=pltpu.VMEM)
PARAMS = pltpu.CompilerParams(vmem_limit_bytes=24 * 1024 * 1024)


def exchange(x, axis, groups=None):
    return lax.all_to_all(
        x, axis, split_axis=0, concat_axis=0, axis_index_groups=groups, tiled=True
    )


def call(kernel, name, out_shape, args):
    return pl.pallas_call(
        kernel,
        out_shape=out_shape,
        in_specs=[VMEM] * len(args),
        out_specs=jax.tree.map(lambda _: VMEM, out_shape),
        compiler_params=PARAMS,
        name=name,
    )(*args)


def per_device(
    queries,
    home_keys,
    home_values,
    home_table,
    home_len,
    lent_keys,
    lent_values,
    lend_row,
    lend_table,
    lend_len,
):
    same_core = [[2 * z + core for z in range(CHIPS)] for core in range(2)]
    plane = [[(2 * z) * N_TP + j for j in range(2 * N_TP)] for z in range(CHIPS)]
    sibling = [(i, i ^ 1) for i in range(N_INST)]
    block = (CHIPS, 4 * ROWS + 8, HD)
    me = jnp.stack([lax.axis_index("inst"), lax.axis_index("tp")]).astype(jnp.int32)
    me = jnp.broadcast_to(me[:, None, None], (2, 8, 128))

    asked = jnp.broadcast_to(lend_row.reshape(N_INST, 2).T.astype(BF16)[:, None], (2, 8, N_INST))
    sent = jnp.concatenate(
        [queries.reshape(2, 8, WIDTH), asked, jnp.zeros((2, 8, 128 - N_INST), BF16)], axis=2
    )
    sent, me = lax.optimization_barrier((sent.reshape(ROWS, WIDTH + 128), me))
    sent = jnp.broadcast_to(sent[None], (N_TP, ROWS, WIDTH + 128))
    first = exchange(sent, "tp")
    sent = pl.pallas_call(
        spread_kernel,
        out_shape=jax.ShapeDtypeStruct(block, BF16),
        in_specs=[VMEM, VMEM],
        out_specs=pl.BlockSpec(memory_space=pl.ANY),
        scratch_shapes=[pltpu.VMEM(block[1:], BF16), pltpu.SemaphoreType.DMA((CHIPS,))],
        compiler_params=PARAMS,
        name="spread",
    )(me, first)
    mine = exchange(sent, "inst", same_core)

    meta = jnp.concatenate(
        [lend_table.reshape(CHIPS, 2, 2, 2), lend_len.reshape(CHIPS, 2, 2, 1)], axis=3
    )
    meta = meta.transpose(3, 1, 0, 2).reshape(3, SLOTS)
    mask = call(
        masks_kernel,
        "masks",
        jax.ShapeDtypeStruct((512, 128), BF16),
        (jnp.concatenate([meta, meta], axis=1),),
    )
    meta = jnp.concatenate([home_table.reshape(ROWS, 1), home_len], axis=1).T
    meta = jnp.pad(meta, ((0, 0), (0, 128 - ROWS)), constant_values=16)
    home, home_lse = call(
        home_kernel,
        "home",
        (
            jax.ShapeDtypeStruct((N_TP, 4 * ROWS, HD), BF16),
            jax.ShapeDtypeStruct((N_TP, ROWS, 128), F32),
        ),
        (meta, first, home_keys, home_values),
    )
    mine, mask, home, home_lse = lax.optimization_barrier((mine, mask, home, home_lse))

    picked, target = call(
        pick_kernel,
        "pick",
        (
            jax.ShapeDtypeStruct((2 * N_TP, HALF, WIDTH), BF16),
            jax.ShapeDtypeStruct((2, 8, 512), F32),
        ),
        (me, mine),
    )
    arrived = exchange(picked, ("inst", "tp"), plane)
    partial = call(
        attend_kernel,
        "attend",
        jax.ShapeDtypeStruct((2 * N_TP, PIECE, HD), BF16),
        (arrived, mask, home, home_lse, lent_keys, lent_values),
    )
    returned = exchange(partial, ("inst", "tp"), plane)
    merged = call(
        merge_kernel, "merge", jax.ShapeDtypeStruct(block, BF16), (target, returned)
    )
    keep, give = call(
        home_merge_kernel,
        "home_merge",
        tuple(jax.ShapeDtypeStruct((ROWS, 4 * HD), F32) for _ in range(2)),
        (me, returned),
    )
    come = lax.ppermute(give, "inst", sibling)
    back = exchange(merged, "inst", same_core)
    return call(
        final_kernel,
        "final",
        jax.ShapeDtypeStruct((ROWS, WIDTH), BF16),
        (me, keep, come, back),
    )


def solution(mesh):
    in_specs = (
        P("inst", "tp"),
        P(("inst", "tp"), None, None),
        P(("inst", "tp"), None, None),
        P("inst", "tp", None),
        P("inst", "tp"),
        P(("inst", "tp"), None, None),
        P(("inst", "tp"), None, None),
        P("inst", None, "tp", None),
        P("inst", None, "tp", None, None),
        P("inst", None, "tp", None),
    )
    out_specs = P("inst", "tp")
    return jax.shard_map(
        per_device, mesh=mesh, in_specs=in_specs, out_specs=out_specs, check_vma=False
    )
```

```python
import functools
import math

import jax
import jax.numpy as jnp
import ml_dtypes
import numpy as np
from jax import lax
from jax.experimental import pallas as pl
from jax.experimental.pallas import tpu as pltpu
from jax.sharding import PartitionSpec as P

QH = 64
KVH = 8
HD = 128
N_INST = 32
N_TP = 16
ROWS = 16
SLOTS = 64
WIDTH = 512
CHIPS = N_INST // 2
HALF = SLOTS // 2
PIECE = 4 * HALF + 2 * ROWS + 8
DEAD = -1e30
SCALE = HD ** (-0.5)
F32 = jnp.float32
BF16 = jnp.bfloat16
FACTOR = SCALE * math.log2(math.e)
TWICE_HI = float(np.float32(1 / FACTOR).astype(ml_dtypes.bfloat16))
TWICE_LO = 1 / FACTOR - TWICE_HI


def iota(shape, axis):
    return lax.broadcasted_iota(jnp.int32, shape, axis)


def dot(a, b):
    return jnp.dot(a, b, preferred_element_type=F32)


def dot_nt(a, b):
    return lax.dot_general(a, b, (((1,), (1,)), ((), ())), preferred_element_type=F32)


def split3(x):
    hi = x.astype(BF16).astype(F32)
    rest = x - hi
    mid = rest.astype(BF16).astype(F32)
    return hi, mid, rest - mid


def thirds(x, lane):
    hi, mid, low = split3(x)
    return jnp.where(lane < 4, hi, jnp.where(lane < 8, mid, jnp.where(lane < 12, low, 0.0)))


def head_rows(h):
    return slice(h * ROWS, (h + 1) * ROWS)


def spread_kernel(me_ref, first_ref, out_ref, block_s, sems):
    row = iota((8, 128), 0)
    quarters = []
    for half in range(2):
        for s in range(2):
            asked = jnp.zeros((8, 128), F32)
            for t in range(8):
                part = first_ref[8 * half + t, :, WIDTH:].astype(F32)
                asked = jnp.where(row == t, part[8 * s : 8 * (s + 1)], asked)
            quarters.append(asked)
    asked = quarters[0]
    for j in range(1, 4):
        asked = asked + pltpu.roll(quarters[j], j * N_INST, 1)
    queries = jnp.zeros((ROWS, WIDTH), F32)
    for t in range(N_TP):
        own = jnp.concatenate([me_ref[1]] * 2, axis=0)[:, :1] == t
        queries = jnp.where(own, first_ref[t, :, :WIDTH].astype(F32), queries)
    queries = queries.astype(BF16)
    for h in range(4):
        block_s[head_rows(h), :] = queries[:, h * HD : (h + 1) * HD]
    block_s[4 * ROWS :, :] = asked.astype(BF16)
    copies = [pltpu.make_async_copy(block_s, out_ref.at[z], sems.at[z]) for z in range(CHIPS)]
    for copy in copies:
        copy.start()
    for copy in copies:
        copy.wait()


def places(me, mine_ref, g):
    k = iota((256, 128), 0)
    n = iota((256, 128), 1)
    local = jnp.bitwise_and(jnp.right_shift(k, 1), 7)
    source = local * 8 + jnp.bitwise_and(jnp.right_shift(k, 4), 7)
    order = jnp.where(n == source, 1.0, 0.0).astype(BF16)
    asked = mine_ref[g * 8 : (g + 1) * 8, 4 * ROWS :, :].astype(F32).reshape(64, 128)
    asked = dot(order[:, :64], asked.astype(BF16))
    column = 2 * N_INST * jnp.right_shift(k, 7) + N_INST * jnp.bitwise_and(k, 1)
    column = column + 2 * jnp.right_shift(me, 1)
    ones = jnp.ones((128, 128), BF16)
    base = local.astype(F32) * 16.0
    return [
        dot(jnp.where(n == column + d, asked, 0.0).astype(BF16), ones) + base
        for d in range(2)
    ]


def pick_kernel(me_ref, mine_ref, out_ref, target_ref):
    lane = iota((256, 128), 1).astype(F32)
    for g in range(2):
        block = jnp.concatenate(
            [
                mine_ref[g * 8 : (g + 1) * 8, head_rows(h), :].reshape(128, HD)
                for h in range(4)
            ],
            axis=1,
        )
        for d, target in enumerate(places(me_ref[0, :1], mine_ref, g)):
            onehot = jnp.where(lane == target, 1.0, 0.0).astype(BF16)
            picked = dot(onehot, block).astype(BF16)
            out_ref[d * N_TP : (d + 1) * N_TP, g * 16 : (g + 1) * 16, :] = picked.reshape(
                N_TP, 16, WIDTH
            )
            target_ref[g, :, d * 256 : (d + 1) * 256] = target.T[:8]


def masks_kernel(lent_ref, out_ref):
    token = iota((512, 128), 0)
    block = jnp.right_shift(token, 4)
    place = jnp.bitwise_and(token, 15)
    length = lent_ref[2:3, :]
    first = (block == lent_ref[0:1, :]) & (place < length)
    other = (block == lent_ref[1:2, :]) & (place + 16 < length)
    twice = first & other
    upper = jnp.where(first | other, jnp.where(twice, TWICE_HI, 0.0), DEAD)
    lower = jnp.where(twice, TWICE_LO, 0.0)
    out_ref[...] = jnp.where(iota((512, 128), 1) < SLOTS, upper, lower).astype(BF16)


HEADS = [(tt, h) for tt in range(2) for h in range(4)]


def pool(query, pick, keys, values, count):
    query = jnp.concatenate([query, jnp.concatenate([pick] * (query.shape[0] // count), axis=0)], axis=1)
    scores = dot_nt(query, keys)
    weights = []
    peaks = []
    for j in range(query.shape[0] // count):
        part = scores[j * count : (j + 1) * count]
        peak = jnp.max(part, axis=1, keepdims=True)
        weights.append(jnp.exp2((part - peak) * FACTOR).astype(BF16))
        peaks.append(peak)
    mixed = dot(jnp.concatenate(weights, axis=0), values)
    total = mixed[:, HD:]
    return (mixed[:, :HD] / total).astype(BF16), peaks, total


def columns(tt, peaks, total, count):
    head = jnp.bitwise_and(iota((count, 128), 1), 3)
    top = jnp.zeros((count, 128), F32)
    amount = jnp.ones((count, 128), F32)
    for h in range(4):
        j = tt * 4 + h
        top = jnp.where(head == h, peaks[j], top)
        amount = jnp.where(head == h, total[j * count : (j + 1) * count], amount)
    return jnp.where(top > DEAD / 2, top * SCALE + jnp.log(amount), DEAD)


def home_kernel(home_ref, first_ref, k_ref, v_ref, out_ref, lse_ref):
    token = iota((256, 128), 0)
    live = (jnp.right_shift(token, 4) == home_ref[0:1, :]) & (
        jnp.bitwise_and(token, 15) < home_ref[1:2, :]
    )
    mask = jnp.where(live, 0.0, DEAD).astype(BF16)
    pick = jnp.where(iota((ROWS, 128), 1) == iota((ROWS, 128), 0), 1.0, 0.0).astype(BF16)
    ones = jnp.ones((256, 128), BF16)
    for k in range(KVH):
        cut = slice(k * HD, (k + 1) * HD)
        keys = jnp.concatenate([k_ref[:, :, cut].reshape(256, HD), mask], axis=1)
        values = jnp.concatenate([v_ref[:, :, cut].reshape(256, HD), ones], axis=1)
        query = [first_ref[2 * k + tt, :, h * HD : (h + 1) * HD] for tt, h in HEADS]
        mixed, peaks, total = pool(jnp.concatenate(query, axis=0), pick, keys, values, ROWS)
        for tt in range(2):
            lse_ref[2 * k + tt] = columns(tt, peaks, total, ROWS)
        for j, (tt, h) in enumerate(HEADS):
            out_ref[2 * k + tt, head_rows(h), :] = mixed[j * ROWS : (j + 1) * ROWS]


def attend_kernel(x_ref, mask_ref, home_ref, home_lse_ref, k_ref, v_ref, out_ref):
    lane = iota((SLOTS, 128), 1)
    pick = jnp.where(
        jnp.bitwise_and(lane, SLOTS - 1) == iota((SLOTS, 128), 0), 1.0, 0.0
    ).astype(BF16)
    mask = mask_ref[...]
    ones = jnp.ones((512, 128), BF16)
    rest = jnp.zeros((ROWS, 128), F32)
    for k in range(KVH):
        cut = slice(k * HD, (k + 1) * HD)
        keys = jnp.concatenate([k_ref[:, :, cut].reshape(512, HD), mask], axis=1)
        values = jnp.concatenate([v_ref[:, :, cut].reshape(512, HD), ones], axis=1)
        for tt in range(2):
            query = [
                x_ref[d * N_TP + 2 * k + tt, :, h * HD : (h + 1) * HD]
                for h in range(4)
                for d in range(2)
            ]
            mixed, peaks, total = pool(jnp.concatenate(query, axis=0), pick, keys, values, SLOTS)
            lse = columns(0, peaks, total, SLOTS)
            home_lse = home_lse_ref[2 * k + tt]
            column = [lse[:HALF], home_lse, rest, lse[HALF:], home_lse, rest]
            lse = thirds(jnp.concatenate(column, axis=0), iota((128, 128), 1)).T
            other = pltpu.roll(lse[:16], 64, 1)
            near = iota((8, 128), 1) < 64
            for d in range(2):
                to = d * N_TP + 2 * k + tt
                for h in range(4):
                    at = h * SLOTS + d * HALF
                    out_ref[to, h * HALF : (h + 1) * HALF, :] = mixed[at : at + HALF]
                out_ref[to, 4 * HALF : PIECE - 8, :] = home_ref[
                    2 * k + tt, 2 * d * ROWS : 2 * (d + 1) * ROWS, :
                ]
                pair = (other[:8], lse[8:16]) if d else (lse[:8], other[8:])
                out_ref[to, PIECE - 8 :, :] = jnp.where(near, *pair).astype(BF16)


def settled(x_ref, groups):
    wide = 2 * len(groups) * 128
    k = iota((128, wide), 0)
    n = iota((128, wide), 1)
    source = 64 * jnp.bitwise_and(jnp.right_shift(n, 7), 1) + jnp.bitwise_and(n, 15)
    for j, group in enumerate(groups):
        source = source + jnp.where(jnp.right_shift(n, 8) == j, 16 * group, 0)
    rows = x_ref[:, PIECE - 8 :, :].astype(F32).reshape(2 * N_TP * 8, 128).astype(BF16)
    moved = dot(rows, jnp.where(k == source, 1.0, 0.0).astype(BF16))
    place = jnp.right_shift(iota((8, 128), 1), 4)

    def settle(chunk, part):
        row = jnp.zeros((8, 128), F32)
        for j in range(8):
            at = (8 * chunk + j) * 8
            row = jnp.where(place == j, moved[at : at + 8, part * 128 : (part + 1) * 128], row)
        return row

    out = []
    for j in range(len(groups)):
        chunks = []
        for chunk in range(4):
            upper = settle(chunk, 2 * j)
            chunks.append(upper[0:4] + upper[4:8] + settle(chunk, 2 * j + 1)[0:4])
        out.append(chunks)
    return out


def join(mask, lse, values):
    score = jnp.where(mask, lse, DEAD)
    peak = jnp.max(score, axis=1, keepdims=True)
    weight = jnp.exp(score - peak)
    upper = weight.astype(BF16)
    lower = (weight - upper.astype(F32)).astype(BF16)
    values = jnp.concatenate([values, jnp.ones(values.shape, BF16)], axis=1)
    both = dot(jnp.concatenate([upper, lower], axis=0), values)
    count = mask.shape[0]
    both = both[:count] + both[count:]
    return both[:, :HD] / both[:, HD:], peak + jnp.log(both[:, HD:])


def merge_kernel(target_ref, x_ref, out_ref):
    lses = settled(x_ref, (0, 1))
    rows = iota((128, 512), 0).astype(F32)
    row = jnp.bitwise_and(iota((128, 128), 0), 8)
    lane = iota((128, 128), 1) - 8 * row
    head = jnp.bitwise_and(lane, 3)
    for g in range(2):
        lse = jnp.concatenate(lses[g], axis=1)
        mask = rows == target_ref[g, 0:1, :]
        out_lse = jnp.zeros((128, 128), F32)
        block = slice(g * 8, (g + 1) * 8)
        for h in range(4):
            at = h * HALF + 16 * g
            values = x_ref[:, at : at + 16, :].reshape(512, HD)
            mixed, total = join(mask, lse[h : h + 1, :], values)
            out_lse = jnp.where(head == h, total, out_lse)
            out_ref[block, head_rows(h), :] = mixed.astype(BF16).reshape(8, ROWS, HD)
        out_lse = jnp.where(lane >= 0, thirds(out_lse, lane), 0.0).reshape(8, ROWS, 128)
        out_ref[block, 4 * ROWS :, :] = (out_lse[:, :8] + out_lse[:, 8:]).astype(BF16)


def home_merge_kernel(me_ref, x_ref, keep_ref, give_ref):
    core = jnp.bitwise_and(me_ref[0, :1], 1)
    lses = settled(x_ref, (2,))[0]
    mask = iota((ROWS, 256), 0) == jnp.bitwise_and(iota((ROWS, 256), 1), 15)
    homes = []
    for d in range(2):
        lse = jnp.concatenate(lses[2 * d : 2 * d + 2], axis=1)
        lse = jnp.where(core[:, :1] == 0, lse[0:2], lse[2:4])
        parts = []
        for hh in range(2):
            at = 4 * HALF + hh * ROWS
            values = x_ref[d * N_TP : (d + 1) * N_TP, at : at + ROWS, :].reshape(256, HD)
            parts.extend(join(mask, lse[hh : hh + 1, :], values))
        homes.append(jnp.concatenate(parts, axis=1))
    keep_ref[...] = jnp.where(core[:, :1] == 0, homes[0], homes[1])
    give_ref[...] = jnp.where(core[:, :1] == 0, homes[1], homes[0])


def final_kernel(me_ref, keep_ref, come_ref, x_ref, out_ref):
    core = jnp.bitwise_and(me_ref[0, :1], 1)
    low = jnp.where(core[:, :1] == 0, keep_ref[...], come_ref[...])
    high = jnp.where(core[:, :1] == 0, come_ref[...], keep_ref[...])
    blocks = [x_ref[c].astype(F32) for c in range(CHIPS)]
    n = iota((128, 1024), 1)
    lane = iota((128, 1024), 0) - 64 * jnp.right_shift(n, 9)
    head = jnp.bitwise_and(jnp.right_shift(n, 7), 3)
    part = (lane >= 0) & (lane < 12) & (jnp.bitwise_and(lane, 3) == head)
    lses = jnp.concatenate([block[4 * ROWS :] for block in blocks], axis=0).astype(BF16)
    lses = dot(lses, jnp.where(part, 1.0, 0.0).astype(BF16))
    for h in range(4):
        home = (low if h < 2 else high)[:, (h % 2) * 2 * HD : (h % 2 + 1) * 2 * HD]
        halves = []
        for half in range(2):
            at = (half * 4 + h) * 128
            rows = slice(half * 8, (half + 1) * 8)
            parts = [lses[c * 8 : (c + 1) * 8, at : at + 128] for c in range(CHIPS)]
            peak = functools.reduce(jnp.maximum, parts, home[rows, HD:])
            total = jnp.exp(home[rows, HD:] - peak)
            mixed = total * home[rows, :HD]
            for c in range(CHIPS):
                weight = jnp.exp(parts[c] - peak)
                total = total + weight
                at = h * ROWS + half * 8
                mixed = mixed + weight * blocks[c][at : at + 8]
            halves.append(mixed / total)
        out_ref[:, h * HD : (h + 1) * HD] = jnp.concatenate(halves, axis=0).astype(BF16)


VMEM = pl.BlockSpec(memory_space=pltpu.VMEM)
PARAMS = pltpu.CompilerParams(vmem_limit_bytes=24 * 1024 * 1024)


def exchange(x, axis, groups=None):
    return lax.all_to_all(
        x, axis, split_axis=0, concat_axis=0, axis_index_groups=groups, tiled=True
    )


def call(kernel, name, out_shape, args):
    return pl.pallas_call(
        kernel,
        out_shape=out_shape,
        in_specs=[VMEM] * len(args),
        out_specs=jax.tree.map(lambda _: VMEM, out_shape),
        compiler_params=PARAMS,
        name=name,
    )(*args)


def per_device(
    queries,
    home_keys,
    home_values,
    home_table,
    home_len,
    lent_keys,
    lent_values,
    lend_row,
    lend_table,
    lend_len,
):
    same_core = [[2 * z + core for z in range(CHIPS)] for core in range(2)]
    plane = [[(2 * z) * N_TP + j for j in range(2 * N_TP)] for z in range(CHIPS)]
    sibling = [(i, i ^ 1) for i in range(N_INST)]
    block = (CHIPS, 4 * ROWS + 8, HD)
    me = jnp.stack([lax.axis_index("inst"), lax.axis_index("tp")]).astype(jnp.int32)
    me = jnp.broadcast_to(me[:, None, None], (2, 8, 128))

    asked = jnp.broadcast_to(lend_row.reshape(N_INST, 2).T.astype(BF16)[:, None], (2, 8, N_INST))
    sent = jnp.concatenate(
        [queries.reshape(2, 8, WIDTH), asked, jnp.zeros((2, 8, 128 - N_INST), BF16)], axis=2
    )
    sent, me = lax.optimization_barrier((sent.reshape(ROWS, WIDTH + 128), me))
    sent = jnp.broadcast_to(sent[None], (N_TP, ROWS, WIDTH + 128))
    first = exchange(sent, "tp")
    sent = pl.pallas_call(
        spread_kernel,
        out_shape=jax.ShapeDtypeStruct(block, BF16),
        in_specs=[VMEM, VMEM],
        out_specs=pl.BlockSpec(memory_space=pl.ANY),
        scratch_shapes=[pltpu.VMEM(block[1:], BF16), pltpu.SemaphoreType.DMA((CHIPS,))],
        compiler_params=PARAMS,
        name="spread",
    )(me, first)
    mine = exchange(sent, "inst", same_core)

    meta = jnp.concatenate(
        [lend_table.reshape(CHIPS, 2, 2, 2), lend_len.reshape(CHIPS, 2, 2, 1)], axis=3
    )
    meta = meta.transpose(3, 1, 0, 2).reshape(3, SLOTS)
    mask = call(
        masks_kernel,
        "masks",
        jax.ShapeDtypeStruct((512, 128), BF16),
        (jnp.concatenate([meta, meta], axis=1),),
    )
    meta = jnp.concatenate([home_table.reshape(ROWS, 1), home_len], axis=1).T
    meta = jnp.pad(meta, ((0, 0), (0, 128 - ROWS)), constant_values=16)
    home, home_lse = call(
        home_kernel,
        "home",
        (
            jax.ShapeDtypeStruct((N_TP, 4 * ROWS, HD), BF16),
            jax.ShapeDtypeStruct((N_TP, ROWS, 128), F32),
        ),
        (meta, first, home_keys, home_values),
    )
    mine, mask, home, home_lse = lax.optimization_barrier((mine, mask, home, home_lse))

    picked, target = call(
        pick_kernel,
        "pick",
        (
            jax.ShapeDtypeStruct((2 * N_TP, HALF, WIDTH), BF16),
            jax.ShapeDtypeStruct((2, 8, 512), F32),
        ),
        (me, mine),
    )
    arrived = exchange(picked, ("inst", "tp"), plane)
    partial = call(
        attend_kernel,
        "attend",
        jax.ShapeDtypeStruct((2 * N_TP, PIECE, HD), BF16),
        (arrived, mask, home, home_lse, lent_keys, lent_values),
    )
    returned = exchange(partial, ("inst", "tp"), plane)
    merged = call(
        merge_kernel, "merge", jax.ShapeDtypeStruct(block, BF16), (target, returned)
    )
    keep, give = call(
        home_merge_kernel,
        "home_merge",
        tuple(jax.ShapeDtypeStruct((ROWS, 4 * HD), F32) for _ in range(2)),
        (me, returned),
    )
    come = lax.ppermute(give, "inst", sibling)
    back = exchange(merged, "inst", same_core)
    return call(
        final_kernel,
        "final",
        jax.ShapeDtypeStruct((ROWS, WIDTH), BF16),
        (me, keep, come, back),
    )


def solution(mesh):
    in_specs = (
        P("inst", "tp"),
        P(("inst", "tp"), None, None),
        P(("inst", "tp"), None, None),
        P("inst", "tp", None),
        P("inst", "tp"),
        P(("inst", "tp"), None, None),
        P(("inst", "tp"), None, None),
        P("inst", None, "tp", None),
        P("inst", None, "tp", None, None),
        P("inst", None, "tp", None),
    )
    out_specs = P("inst", "tp")
    return jax.shard_map(
        per_device, mesh=mesh, in_specs=in_specs, out_specs=out_specs, check_vma=False
    )
```
